512 devices in a mesh: row: 16 (over z), col: 32 (over x, y, core).
Axes of the slice: x: 4, y: 4, z: 16, core: 2. Of those that a mesh axis runs over, the one named last changes fastest.
Arguments:
- left_factors: bfloat16 [96, 96, 96, 512], P('row', 'col'), may hold values from -6 to 6
- right_factors: bfloat16 [96, 96, 96, 512], P('row', 'col'), may hold values from -0.015625 to 0.015625
- ranks: int32 [96, 96], P('row', 'col'), may hold values from 16 to 96
- sketch_left: bfloat16 [96, 128, 512], P('row'), may hold values from -32 to 32
- sketch_right: bfloat16 [512, 128], replicated, may hold values from -32 to 32
- upper_inverse: bfloat16 [512, 512], replicated, as said below
- step: int32 [1], replicated, may hold values from 48 to 94
Outputs:
- range_sketch: bfloat16 [96, 128, 512], P('row')
- factored_sketch: bfloat16 [96, 128, 512], P('row')
The draws below stay inside these ranges and needn't reach their ends.
Inputs may be any that keep to these rules, and one draw needn't show every extreme that they name: `ranks`: rows of a tile's factors at or beyond its rank are not part of the tile. `step`: columns before this one are factored. `upper_inverse`: upper triangular.
All inputs are finite; a program needn't handle non-finite values.
Results may differ from the reference program's by a relative error of at most 0.0071.
Values may be sent and summed in bfloat16 or wider, within the bound.
A program may use at most 64 MiB of HBM per device.

```python
import jax
import jax.numpy as jnp
from jax import lax

TILE = 512
RMAX = 96
SKETCH = 128
NT = 96


def draw_upper_inverse(key, part):
    key = jax.random.fold_in(key, 7)
    key_off, key_diag = jax.random.split(key)
    row_ids = jnp.arange(TILE, dtype=jnp.int32)[:, None]
    col_ids = jnp.arange(TILE, dtype=jnp.int32)[None, :]
    spread = 0.02 * jax.random.normal(key_off, (TILE, TILE), jnp.float32)
    diag_vals = jax.random.uniform(key_diag, (TILE,), jnp.float32, 1.0, 2.0)
    upper = jnp.where(col_ids > row_ids, spread, jnp.float32(0.0))
    upper = upper + jnp.where(col_ids == row_ids, diag_vals[None, :], jnp.float32(0.0))
    return upper.astype(jnp.bfloat16)


def touch_ends(entries, stream_key, least, largest):
    longest = entries.shape.index(max(entries.shape))
    spots = []
    for shift in (0, 1):
        where = [jax.random.randint(jax.random.fold_in(stream_key, axis), (), 0, length) for axis, length in enumerate(entries.shape)]
        where[longest] = (where[longest] + shift) % entries.shape[longest]
        spots.append(tuple(where))
    return entries.at[spots[0]].set(least).at[spots[1]].set(largest)


def steps_of(rng, dims, cuts, least, high):
    def one(position, parts):
        heights = jax.random.uniform(jax.random.fold_in(jax.random.fold_in(rng, 6), position), (parts,), jnp.float32, least / len(cuts), high / len(cuts))
        return jnp.repeat(jnp.exp(heights), dims[position] // parts).reshape((-1,) + (1,) * (len(dims) - position - 1))

    level = one(*cuts[0])
    for cut in cuts[1:]:
        level = level * one(*cut)
    return level


def bell_draw(rng, shape, scale, most, cuts=(), kind=jnp.bfloat16):
    drawn = scale * jax.random.normal(rng, shape, jnp.float32)
    if cuts:
        drawn = drawn * steps_of(rng, shape, cuts, -0.22, 0.18)
    return jnp.clip(drawn, -most, most).astype(kind)


def setup_inputs(seed: int = 0) -> dict:
    arg_keys = jax.random.split(jax.random.key(seed), 8)
    return {
        "left_factors": bell_draw(arg_keys[0], (NT, NT, RMAX, TILE), 1.0, 6.0, ((0, 16), (1, 32))),
        "right_factors": bell_draw(arg_keys[1], (NT, NT, RMAX, TILE), (1.0 / (2 * TILE)), 0.015625, ((0, 16), (1, 32))),
        "ranks": touch_ends(jax.random.randint(arg_keys[2], (NT, NT), RMAX // 6, RMAX + 1), jax.random.fold_in(arg_keys[2], 1), RMAX // 6, RMAX).astype(jnp.int32),
        "sketch_left": bell_draw(arg_keys[3], (NT, SKETCH, TILE), 5.0, 32.0, ((0, 16),)),
        "sketch_right": bell_draw(arg_keys[4], (TILE, SKETCH), 5.0, 32.0),
        "upper_inverse": draw_upper_inverse(jax.random.fold_in(arg_keys[7], 71), 0),
        "step": jax.random.randint(arg_keys[6], (1,), NT // 2, NT - 1).astype(jnp.int32),
    }


def reference(left_factors, right_factors, ranks, sketch_left, sketch_right, upper_inverse, step):
    column = step[0]
    high = lax.Precision.HIGHEST
    levels = jnp.arange(RMAX, dtype=jnp.int32)
    col_left = lax.dynamic_index_in_dim(left_factors, column, 1, keepdims=False)
    col_rank = lax.dynamic_index_in_dim(ranks, column, 1, keepdims=False)
    col_left = jnp.where(levels[None, :, None] < col_rank[:, None, None], col_left, jnp.zeros_like(col_left))
    col_right = lax.dynamic_index_in_dim(right_factors, column, 1, keepdims=False)
    col_left_f = col_left.astype(jnp.float32)
    col_right_f = col_right.astype(jnp.float32)
    reduced = jnp.einsum('jrt,tp->jrp', col_right_f, sketch_right.astype(jnp.float32), precision=high).astype(jnp.bfloat16)
    reduced_f = reduced.astype(jnp.float32)
    col_ids = jnp.arange(NT, dtype=jnp.int32)

    def one_row(row_index):
        left_row = lax.dynamic_index_in_dim(left_factors, row_index, 0, keepdims=False)
        rank_row = lax.dynamic_index_in_dim(ranks, row_index, 0, keepdims=False)
        left_row = jnp.where(levels[None, :, None] < rank_row[:, None, None], left_row, jnp.zeros_like(left_row))
        left_row_f = left_row.astype(jnp.float32)
        right_row = lax.dynamic_index_in_dim(right_factors, row_index, 0, keepdims=False).astype(jnp.float32)
        sketch_row = lax.dynamic_index_in_dim(sketch_left, row_index, 0, keepdims=False).astype(jnp.float32)
        coupling = jnp.einsum('jrt,jst->jrs', right_row, col_left_f, precision=high).astype(jnp.bfloat16).astype(jnp.float32)
        active = (row_index > column) & (col_ids < column)
        mixed = jnp.einsum('jrs,jsp->jrp', coupling, reduced_f, precision=high)
        mixed = jnp.where(active[:, None, None], mixed, jnp.float32(0.0)).astype(jnp.bfloat16)
        range_terms = jnp.einsum('jrp,jrt->pt', mixed.astype(jnp.float32), left_row_f, precision=high)
        probe_left = jnp.einsum('pt,jrt->jpr', sketch_row, left_row_f, precision=high).astype(jnp.bfloat16).astype(jnp.float32)
        folded = jnp.einsum('jpr,jrs->jps', probe_left, coupling, precision=high)
        folded = jnp.where(active[:, None, None], folded, jnp.float32(0.0)).astype(jnp.bfloat16)
        co_terms = jnp.einsum('jps,jst->pt', folded.astype(jnp.float32), col_right_f, precision=high)
        weight = (row_index > column).astype(jnp.float32)
        own_reduced = lax.dynamic_index_in_dim(reduced_f, row_index, 0, keepdims=False)
        own_left = lax.dynamic_index_in_dim(col_left_f, row_index, 0, keepdims=False)
        own_right = lax.dynamic_index_in_dim(col_right_f, row_index, 0, keepdims=False)
        own_range = jnp.einsum('rp,rt->pt', own_reduced, own_left, precision=high)
        own_probe = jnp.einsum('pt,rt->pr', sketch_row, own_left, precision=high).astype(jnp.bfloat16)
        own_co = jnp.einsum('pr,rt->pt', own_probe.astype(jnp.float32), own_right, precision=high)
        return weight * own_range - range_terms, weight * own_co - co_terms

    range_sum, co_sum = lax.map(one_row, jnp.arange(NT, dtype=jnp.int32))
    range_sketch = range_sum.astype(jnp.bfloat16)
    factored = jnp.einsum('ipt,ts->ips', co_sum.astype(jnp.bfloat16).astype(jnp.float32), upper_inverse.astype(jnp.float32), precision=high)
    return range_sketch, factored.astype(jnp.bfloat16)
```

```python
import functools

import jax
import jax.numpy as jnp
from jax import lax
from jax.experimental import pallas as pl
from jax.experimental.pallas import tpu as pltpu
from jax.sharding import PartitionSpec as P

MESH = pl.DeviceIdType.MESH
F32 = jnp.float32
BF16 = jnp.bfloat16
FIRST = 8
LAST = 15
HALF = 48
CHUNKS = 12


def remote(src, dst, send_sem, recv_sem, device):
    return pltpu.make_async_remote_copy(
        src_ref=src,
        dst_ref=dst,
        send_sem=send_sem,
        recv_sem=recv_sem,
        device_id=device,
        device_id_type=MESH,
    )


def gather_kernel(ranks_ref, step_ref, left_ref, right_ref, panel_ref, sems):
    column = step_ref[0]
    slot = lax.rem(column, 3)

    @pl.when(lax.axis_index("col") == column // 3)
    def _():
        copies = [
            pltpu.make_async_copy(left_ref.at[:, slot], panel_ref.at[:, 0], sems.at[0]),
            pltpu.make_async_copy(right_ref.at[:, slot], panel_ref.at[:, 1], sems.at[1]),
        ]
        for copy in copies:
            copy.start()
        for copy in copies:
            copy.wait()
        level = lax.broadcasted_iota(jnp.int32, (96, 512), 0)
        for i in range(6):
            tile = panel_ref[i, 0]
            panel_ref[i, 0] = jnp.where(level < ranks_ref[slot, i], tile, jnp.zeros_like(tile))


def gather_panel(ranks, step, left, right):
    return pl.pallas_call(
        gather_kernel,
        out_shape=jax.ShapeDtypeStruct((6, 2, 96, 512), BF16),
        in_specs=[
            pl.BlockSpec(memory_space=pltpu.SMEM),
            pl.BlockSpec(memory_space=pltpu.SMEM),
            pl.BlockSpec(memory_space=pl.ANY),
            pl.BlockSpec(memory_space=pl.ANY),
        ],
        out_specs=pl.BlockSpec(memory_space=pltpu.VMEM),
        scratch_shapes=[pltpu.SemaphoreType.DMA((2,))],
        compiler_params=pltpu.CompilerParams(vmem_limit_bytes=62 * 2**20),
        name="gather_panel",
    )(ranks, step, left, right)


def panel_kernel(
    owner, panel_ref, out_ref, extra_ref, src_send, up_send, down_send, recv_sem,
    extra_up, extra_down, extra_recv, give_send, local_sem,
):
    z = lax.axis_index("row")
    c = lax.axis_index("col")
    s = c // 2
    kind = c % 2
    owner_line = owner // 2
    owner_core = owner % 2
    carrier = owner + 1 - 2 * owner_core
    low = s < FIRST
    high = jnp.logical_not(low)
    home = z == s
    is_owner = c == owner
    is_carrier = c == carrier
    target = z >= FIRST
    way = (c == 0) & (z == 4)
    up = (low & (kind == 0) & (home | way | (target & (z < LAST)))) | (high & (z >= s) & (z < LAST))
    down = (low & (kind == 1) & (home | (z > FIRST))) | (high & (z <= s) & (z > FIRST))
    up = up & jnp.logical_not(is_owner)
    down = down & jnp.logical_not(is_owner)
    up_to = jnp.where((c == 0) & (z == 0), 4, jnp.where(z < FIRST, FIRST, z + 1))
    down_to = jnp.where(z < FIRST, LAST, z - 1)
    from_owner = home & jnp.logical_not(is_owner)
    from_below = ((low & (kind == 0)) | (high & (z > s))) & target | way
    from_above = ((low & (kind == 1)) | (high & (z < s))) & target
    from_below = from_below & jnp.logical_not(is_owner)
    from_above = from_above & jnp.logical_not(is_owner)
    entry = jnp.where(c == 0, 4, s)
    below = jnp.where(way, 0, jnp.where(low & (z == FIRST), entry, z - 1))
    above = jnp.where(low & (z == LAST), s, z + 1)
    from_carrier = is_owner & target & (z != owner_line)
    receives = from_owner | from_below | from_above | from_carrier
    sends_home = is_owner & (z != owner_line)
    holds_own = is_owner & (z == owner_line)
    carries = is_carrier & target

    barrier = pltpu.get_barrier_semaphore()

    def greet(flag, device):
        @pl.when(flag)
        def _():
            pl.semaphore_signal(barrier, inc=1, device_id=device, device_id_type=MESH)

    greet(from_owner, (z, owner))
    greet(from_below, (below, c))
    greet(from_above, (above, c))
    greet(from_carrier, (z, carrier))

    def count(flag, amount=1):
        return jnp.where(flag, amount, 0)

    peers = (
        count(is_owner, jnp.where(z == owner_line, 1, 2))
        + count(up)
        + count(down)
        + count(carries & (z != owner_line))
    )

    @pl.when(peers > 0)
    def _():
        pl.semaphore_wait(barrier, peers)

    def piece(q):
        return q // 4, (q // 2) % 2, pl.ds(pl.multiple_of((q % 2) * HALF, HALF), HALF)

    def src_copy(core, q):
        t, side, rows = piece(q)
        return remote(
            panel_ref.at[3 * core + t, side, rows],
            out_ref.at[t, side, rows],
            src_send.at[core, q],
            recv_sem.at[q],
            (z, 2 * z + core),
        )

    def lend_copy(q):
        t, side, rows = piece(q)
        return remote(
            panel_ref.at[3 * owner_core + t, side, rows],
            extra_ref.at[t, side, rows],
            src_send.at[owner_core, q],
            extra_recv.at[q],
            (z, carrier),
        )

    def chain_copy(ref, send, recv, device, q):
        t, side, rows = piece(q)
        here = ref.at[t, side, rows]
        return remote(here, here, send.at[q], recv.at[q], device)

    def give_copy(q):
        t, side, rows = piece(q)
        return remote(
            extra_ref.at[t, side, rows], out_ref.at[t, side, rows], give_send.at[q], recv_sem.at[q], (z, owner)
        )

    def up_copy(q):
        return chain_copy(out_ref, up_send, recv_sem, (up_to, c), q)

    def down_copy(q):
        return chain_copy(out_ref, down_send, recv_sem, (down_to, c), q)

    def extra_up_copy(q):
        return chain_copy(extra_ref, extra_up, extra_recv, (z + 1, c), q)

    def extra_down_copy(q):
        return chain_copy(extra_ref, extra_down, extra_recv, (z - 1, c), q)

    def loop(flag, body):
        @pl.when(flag)
        def _():
            lax.fori_loop(0, CHUNKS, lambda q, _: (body(q), 0)[1], 0)

    def when(flag, body):
        @pl.when(flag)
        def _():
            body()

    loop(holds_own, lambda q: lend_copy(q).start())
    for core in range(2):
        flag = is_owner if core != owner_core else sends_home
        loop(flag, lambda q, core=core: src_copy(core, q).start())

    @pl.when(holds_own)
    def _():
        copy = pltpu.make_async_copy(panel_ref.at[pl.ds(3 * owner_core, 3)], out_ref, local_sem)
        copy.start()
        copy.wait()

    def relay(q):
        when(receives, lambda: chain_copy(out_ref, up_send, recv_sem, (z, c + 1 - 2 * kind), q).wait_recv())
        when(up, lambda: up_copy(q).start())
        when(down, lambda: down_copy(q).start())

        @pl.when(carries)
        def _():
            chain_copy(extra_ref, extra_up, extra_recv, (z, owner), q).wait_recv()
            when((z >= owner_line) & (z < LAST), lambda: extra_up_copy(q).start())
            when((z <= owner_line) & (z > FIRST), lambda: extra_down_copy(q).start())
            when(z != owner_line, lambda: give_copy(q).start())

    lax.fori_loop(0, CHUNKS, lambda q, _: (relay(q), 0)[1], 0)

    loop(holds_own, lambda q: lend_copy(q).wait_send())
    for core in range(2):
        flag = is_owner if core != owner_core else sends_home
        loop(flag, lambda q, core=core: src_copy(core, q).wait_send())
    loop(up, lambda q: up_copy(q).wait_send())
    loop(down, lambda q: down_copy(q).wait_send())
    loop(carries & (z >= owner_line) & (z < LAST), lambda q: extra_up_copy(q).wait_send())
    loop(carries & (z <= owner_line) & (z > FIRST), lambda q: extra_down_copy(q).wait_send())
    loop(carries & (z != owner_line), lambda q: give_copy(q).wait_send())


def spread_panel(owner, panel):
    return pl.pallas_call(
        functools.partial(panel_kernel, owner),
        out_shape=jax.ShapeDtypeStruct((3, 2, 96, 512), BF16),
        in_specs=[pl.BlockSpec(memory_space=pltpu.VMEM)],
        out_specs=pl.BlockSpec(memory_space=pltpu.VMEM),
        scratch_shapes=[
            pltpu.VMEM((3, 2, 96, 512), BF16),
            pltpu.SemaphoreType.DMA((2, CHUNKS)),
            pltpu.SemaphoreType.DMA((CHUNKS,)),
            pltpu.SemaphoreType.DMA((CHUNKS,)),
            pltpu.SemaphoreType.DMA((CHUNKS,)),
            pltpu.SemaphoreType.DMA((CHUNKS,)),
            pltpu.SemaphoreType.DMA((CHUNKS,)),
            pltpu.SemaphoreType.DMA((CHUNKS,)),
            pltpu.SemaphoreType.DMA((CHUNKS,)),
            pltpu.SemaphoreType.DMA,
        ],
        compiler_params=pltpu.CompilerParams(
            collective_id=owner - 15, has_side_effects=True, vmem_limit_bytes=16 * 2**20
        ),
        name="spread_panel",
    )(panel)


def dot_nt(a, b):
    return lax.dot_general(a, b, (((1,), (1,)), ((), ())), preferred_element_type=F32)


def dot_nn(a, b):
    return jnp.dot(a, b, preferred_element_type=F32)


def row_kernel(
    ranks_ref, step_ref, left_hbm, right_hbm, probe_hbm, upper_ref, sketch_ref, solve_ref, out_ref,
    left_ref, right_ref, probe_ref, stack_ref, reduced_ref,
    send_ref, got_ref, acc_ref, cur_ref, a1_ref, a2_ref, b_ref, blk_ref,
    load_sem, send_sem, recv_sem, b_send, b_recv, pair_send, pair_recv,
):
    z = lax.axis_index("row")
    c = lax.axis_index("col")
    x = c // 8
    y = (c // 2) % 4
    core = c % 2
    sibling = (z, c + 1 - 2 * core)
    place = (x, y)
    order = (0, 3, 1, 4, 2, 5)

    def near(axis, by):
        if axis == 0:
            return (z, ((x + by + 4) % 4) * 8 + y * 2 + core)
        return (z, x * 8 + ((y + by + 4) % 4) * 2 + core)

    def rows32(b):
        return pl.ds(pl.multiple_of(((b + 4) % 4) * 32, 32), 32)

    def rows16(b, h):
        return pl.ds(pl.multiple_of(((b + 4) % 4) * 32 + 16 * h, 16), 16)

    def cols(b):
        return pl.ds(pl.multiple_of(((b + 4) % 4) * 128, 128), 128)

    def axes(a):
        return (0, 1) if a < 3 else (1, 0)

    def two_ways(a, n, src, dst):
        axis = axes(a)[0]
        return [
            remote(src(d), dst(d), send_sem.at[a, n, d], recv_sem.at[a, n, d], near(axis, 1 - 2 * d))
            for d in range(2)
        ]

    def copies(a, n):
        first, second = axes(a)
        u, v = place[first], place[second]
        mine = out_ref.at[core, a]
        if n == 0:
            return two_ways(a, 0, lambda d: cur_ref.at[a, rows16(u + 2, d)], lambda d: a1_ref.at[a, d])
        if n == 1:
            return two_ways(a, 1, lambda d: cur_ref.at[a, rows32(u + 1 - 2 * d)], lambda d: a2_ref.at[a, d])
        if n == 2:
            return [
                remote(
                    cur_ref.at[a, rows32(u), cols(v + by)], b_ref.at[a, by - 1],
                    b_send.at[a, 0, by - 1], b_recv.at[a, 0, by - 1], near(second, by),
                )
                for by in (1, 2, 3)
            ]
        if n == 3:
            block = blk_ref.at[a, :, cols(v)]
            return [
                remote(block, block, b_send.at[a, 1, by - 1], b_recv.at[a, 1, by - 1], near(second, by))
                for by in (1, 2, 3)
            ]
        if n == 4:
            block = mine.at[rows32(u)]
            return two_ways(a, 2, lambda d: block, lambda d: block)

        def half(d):
            return mine.at[rows16(u - 1 + 2 * d, d)]

        return two_ways(a, 3, half, half)

    def pair_copy(a):
        return remote(send_ref.at[a], got_ref.at[a], pair_send.at[0, a], pair_recv.at[0, a], sibling)

    def give_copy(a, which):
        here = out_ref.at[which, a]
        return remote(here, here, pair_send.at[1, a], pair_recv.at[1, a], sibling)

    def loads(a):
        return [
            pltpu.make_async_copy(left_hbm.at[a], left_ref.at[a], load_sem.at[0, a]),
            pltpu.make_async_copy(right_hbm.at[a], right_ref.at[a], load_sem.at[1, a]),
            pltpu.make_async_copy(probe_hbm.at[a], probe_ref.at[a], load_sem.at[2, a]),
        ]

    def start(a, n):
        for copy in copies(a, n):
            copy.start()

    def arrive(a, n):
        for copy in copies(a, n):
            copy.wait_recv()

    def compute(a):
        column = step_ref[0]
        for copy in loads(a):
            copy.wait()
        level = lax.broadcasted_iota(jnp.int32, (128, 96), 1)
        live = z * 6 + a > column
        range_sum = jnp.zeros((128, 512), F32)
        co_sum = jnp.zeros((128, 512), F32)
        for j in range(3):
            tile = c * 3 + j
            own = tile == column
            depth = jnp.where(live & (tile <= column), ranks_ref[j, a], 0)
            keep = level < depth
            left = left_ref[a, j]
            right = right_ref[a, j]
            both = dot_nt(stack_ref[j], right)
            coupled = both[:96].astype(BF16)
            mixed = dot_nn(reduced_ref[j], coupled)
            mixed = jnp.where(own, -both[96:], mixed)
            mixed = jnp.where(keep, mixed, 0.0).astype(BF16)
            probed = dot_nt(probe_ref[a], left)
            probed = jnp.where(keep, probed, 0.0).astype(BF16)
            folded = dot_nt(probed, coupled).astype(BF16)
            folded = jnp.where(own, -probed, folded)
            closing = jnp.where(own, right, upper_ref[j, 1])
            range_sum += dot_nn(mixed, left)
            co_sum += dot_nn(folded, closing)
        even = core == 0
        acc_ref[a] = -jnp.where(even, range_sum, co_sum)
        send_ref[a] = -jnp.where(even, co_sum, range_sum).astype(BF16)
        pair_copy(a).start()

    def stage(n, a):
        first, second = axes(a)
        u, v = place[first], place[second]
        if n == 0:
            pair_copy(a).wait_recv()
            acc_ref[a] += got_ref[a].astype(F32)
            cur_ref[a, rows32(u + 2)] = acc_ref[a, rows32(u + 2)].astype(BF16)
            start(a, 0)
        elif n == 1:
            arrive(a, 0)
            for d in range(2):
                near_rows = rows32(u + 1 - 2 * d)
                rows = rows16(u + 1 - 2 * d, d)
                acc_ref[a, rows] += a1_ref[a, d].astype(F32)
                cur_ref[a, near_rows] = acc_ref[a, near_rows].astype(BF16)
            start(a, 1)
        elif n == 2:
            arrive(a, 1)
            rows = rows32(u)
            total = acc_ref[a, rows] + a2_ref[a, 0].astype(F32) + a2_ref[a, 1].astype(F32)
            acc_ref[a, rows] = total
            cur_ref[a, rows] = total.astype(BF16)
            start(a, 2)
        elif n == 3:
            arrive(a, 2)
            total = acc_ref[a, rows32(u), cols(v)]
            for d in range(3):
                total += b_ref[a, d].astype(F32)
            blk_ref[a, :, cols(v)] = total.astype(BF16)
            start(a, 3)
        elif n == 4:
            for by in (1, 2, 3):
                theirs = blk_ref.at[a, :, cols(v - by)]
                remote(
                    theirs, theirs, b_send.at[a, 1, by - 1], b_recv.at[a, 1, by - 1], near(second, by)
                ).wait_recv()

            @pl.when(core == 0)
            def _():
                out_ref[0, a, rows32(u)] = blk_ref[a]

            @pl.when(core == 1)
            def _():
                out_ref[1, a, rows32(u)] = dot_nn(blk_ref[a], solve_ref[...]).astype(BF16)

            start(a, 4)
        elif n == 5:
            arrive(a, 4)
            start(a, 5)
        elif n == 6:
            arrive(a, 5)
            give_copy(a, core).start()
        else:
            give_copy(a, 1 - core).wait_recv()

    @pl.when(z < FIRST)
    def _():
        out_ref[...] = jnp.zeros_like(out_ref)

    @pl.when(z >= FIRST)
    def _():
        for a in order:
            for copy in loads(a):
                copy.start()
        barrier = pltpu.get_barrier_semaphore()
        peers = (sibling, near(0, 1), near(0, 2), near(0, 3), near(1, 1), near(1, 2), near(1, 3))
        for device in peers:
            pl.semaphore_signal(barrier, inc=1, device_id=device, device_id_type=MESH)
        flat = sketch_ref[...].astype(F32).T.astype(BF16)
        for j in range(3):
            stack_ref[j, :96] = upper_ref[j, 0]
            stack_ref[j, 96:] = flat
            reduced = dot_nn(upper_ref[j, 1], sketch_ref[...]).astype(BF16).astype(F32)
            reduced_ref[j] = reduced.T.astype(BF16)
        pl.semaphore_wait(barrier, 7)
        for t in range(15):
            if t < 6:
                compute(order[t])
            for n in reversed(range(8)):
                if 0 <= t - 1 - n < 6:
                    stage(n, order[t - 1 - n])
        for a in range(6):
            pair_copy(a).wait_send()
            give_copy(a, core).wait_send()
            for n in range(6):
                for copy in copies(a, n):
                    copy.wait_send()


def row_sums(ranks, step, left, right, probes, upper, sketch, solve):
    vmem = pl.BlockSpec(memory_space=pltpu.VMEM)
    smem = pl.BlockSpec(memory_space=pltpu.SMEM)
    hbm = pl.BlockSpec(memory_space=pl.ANY)
    return pl.pallas_call(
        row_kernel,
        out_shape=jax.ShapeDtypeStruct((2, 6, 128, 512), BF16),
        in_specs=[smem, smem, hbm, hbm, hbm, vmem, vmem, vmem],
        out_specs=vmem,
        scratch_shapes=[
            pltpu.VMEM((6, 3, 96, 512), BF16),
            pltpu.VMEM((6, 3, 96, 512), BF16),
            pltpu.VMEM((6, 128, 512), BF16),
            pltpu.VMEM((3, 224, 512), BF16),
            pltpu.VMEM((3, 128, 96), BF16),
            pltpu.VMEM((6, 128, 512), BF16),
            pltpu.VMEM((6, 128, 512), BF16),
            pltpu.VMEM((6, 128, 512), F32),
            pltpu.VMEM((6, 128, 512), BF16),
            pltpu.VMEM((6, 2, 16, 512), BF16),
            pltpu.VMEM((6, 2, 32, 512), BF16),
            pltpu.VMEM((6, 3, 32, 128), BF16),
            pltpu.VMEM((6, 32, 512), BF16),
            pltpu.SemaphoreType.DMA((3, 6)),
            pltpu.SemaphoreType.DMA((6, 4, 2)),
            pltpu.SemaphoreType.DMA((6, 4, 2)),
            pltpu.SemaphoreType.DMA((6, 2, 3)),
            pltpu.SemaphoreType.DMA((6, 2, 3)),
            pltpu.SemaphoreType.DMA((2, 6)),
            pltpu.SemaphoreType.DMA((2, 6)),
        ],
        compiler_params=pltpu.CompilerParams(
            collective_id=0, has_side_effects=True, vmem_limit_bytes=62 * 2**20
        ),
        name="row_sums",
    )(ranks, step, left, right, probes, upper, sketch, solve)


def body(left_factors, right_factors, ranks, sketch_left, sketch_right, upper_inverse, step):
    slots = ranks.T
    panel = gather_panel(slots, step, left_factors, right_factors)
    branches = [functools.partial(spread_panel, owner) for owner in range(16, 32)]
    upper = lax.switch(lax.div(step[0], 3) - 16, branches, panel)
    out = row_sums(
        slots, step, left_factors, right_factors, sketch_left, upper, sketch_right, upper_inverse
    )
    return (out[0], out[1])


def solution(mesh):
    return jax.shard_map(
        body,
        mesh=mesh,
        in_specs=(
            P("row", "col", None, None),
            P("row", "col", None, None),
            P("row", "col"),
            P("row", None, None),
            P(),
            P(),
            P(),
        ),
        out_specs=(P("row", None, None), P("row", None, None)),
        check_vma=False,
    )
```

```python
import functools

import jax
import jax.numpy as jnp
from jax import lax
from jax.experimental import pallas as pl
from jax.experimental.pallas import tpu as pltpu
from jax.sharding import PartitionSpec as P

MESH = pl.DeviceIdType.MESH
F32 = jnp.float32
BF16 = jnp.bfloat16
FIRST = 8
LAST = 15
HALF = 48
CHUNKS = 12


def remote(src, dst, send_sem, recv_sem, device):
    return pltpu.make_async_remote_copy(
        src_ref=src,
        dst_ref=dst,
        send_sem=send_sem,
        recv_sem=recv_sem,
        device_id=device,
        device_id_type=MESH,
    )


def line_trees():
    trees = []
    for s in range(16):
        parent = {}

        def chain(*planes):
            for before, after in zip(planes, planes[1:]):
                parent[after] = before

        low = s < FIRST
        if low or s == 15:
            chain(*((s, 4, 9) if s < 2 else (s, 5, 9) if s == 15 else (s, 9)), 10, 11)
            chain(9, 8)
        if low or s == 8:
            chain(*((s, 3, 14) if 6 <= s < 8 else (s, 2, 14) if s == 8 else (s, 14)), 13, 12)
            chain(14, 15)
        if s == 8:
            chain(8, 9, 10, 11)
        if s == 15:
            chain(15, 14, 13, 12)
        if s == 9:
            chain(9, 10, 11, 12, 13)
            chain(9, 8, 2, 15, 14)
        if s == 14:
            chain(14, 13, 12, 11, 10)
            chain(14, 15, 5, 8, 9)
        if 10 <= s <= 13:
            chain(*range(s, 16))
            chain(*range(s, 7, -1))
        trees.append(parent)
    return trees


def table_words(entries):
    return [
        sum(entries[s][4 * w + d] * 16**d for d in range(4)) for s in range(16) for w in range(4)
    ]


def tree_tables():
    none = [list(range(16)) for _ in range(16)]
    parents = [list(row) for row in none]
    firsts = [list(row) for row in none]
    seconds = [list(row) for row in none]
    for s, tree in enumerate(line_trees()):
        for plane, before in tree.items():
            parents[s][plane] = before
            if firsts[s][before] == before:
                firsts[s][before] = plane
            else:
                assert seconds[s][before] == before
                seconds[s][before] = plane
    return [table_words(entries) for entries in (parents, firsts, seconds)]


def look_up(words, s, z):
    index = s * 4 + z // 4
    word = words[0]
    for k, value in enumerate(words):
        if k:
            word = jnp.where(index == k, value, word)
    digit = z % 4
    scale = jnp.where(digit == 0, 1, jnp.where(digit == 1, 16, jnp.where(digit == 2, 256, 4096)))
    return (word // scale) % 16


def gather_kernel(ranks_ref, step_ref, left_ref, right_ref, panel_ref, sems):
    column = step_ref[0]
    slot = lax.rem(column, 3)

    @pl.when(lax.axis_index("col") == column // 3)
    def _():
        copies = [
            pltpu.make_async_copy(left_ref.at[:, slot], panel_ref.at[:, 0], sems.at[0]),
            pltpu.make_async_copy(right_ref.at[:, slot], panel_ref.at[:, 1], sems.at[1]),
        ]
        for copy in copies:
            copy.start()
        for copy in copies:
            copy.wait()
        level = lax.broadcasted_iota(jnp.int32, (96, 512), 0)
        for i in range(6):
            tile = panel_ref[i, 0]
            panel_ref[i, 0] = jnp.where(level < ranks_ref[slot, i], tile, jnp.zeros_like(tile))


def gather_panel(ranks, step, left, right):
    return pl.pallas_call(
        gather_kernel,
        out_shape=jax.ShapeDtypeStruct((6, 2, 96, 512), BF16),
        in_specs=[
            pl.BlockSpec(memory_space=pltpu.SMEM),
            pl.BlockSpec(memory_space=pltpu.SMEM),
            pl.BlockSpec(memory_space=pl.ANY),
            pl.BlockSpec(memory_space=pl.ANY),
        ],
        out_specs=pl.BlockSpec(memory_space=pltpu.VMEM),
        scratch_shapes=[pltpu.SemaphoreType.DMA((2,))],
        compiler_params=pltpu.CompilerParams(vmem_limit_bytes=62 * 2**20),
        name="gather_panel",
    )(ranks, step, left, right)


def panel_kernel(
    owner, panel_ref, out_ref, extra_ref, src_send, up_send, down_send, recv_sem,
    extra_up_send, extra_down_send, extra_recv, give_send, local_sem,
):
    z = lax.axis_index("row")
    c = lax.axis_index("col")
    s = c // 2
    kind = c % 2
    owner_line = owner // 2
    owner_core = owner % 2
    carrier = owner + 1 - 2 * owner_core
    home = z == s
    is_owner = c == owner
    is_carrier = c == carrier
    target = z >= FIRST
    parent, first, second = (look_up(words, s, z) for words in tree_tables())
    plain = jnp.logical_not(is_owner)
    up = plain & (first != z)
    down = plain & (second != z)
    from_owner = home & plain
    from_parent = plain & (parent != z)
    from_carrier = is_owner & target & (z != owner_line)
    receives = from_owner | from_parent | from_carrier
    sends_home = is_owner & (z != owner_line)
    holds_own = is_owner & (z == owner_line)
    extra_up = is_carrier & (first != z)
    extra_down = is_carrier & (second != z)
    extra_gives = is_carrier & target & (z != owner_line)
    extra_takes = is_carrier & (home | (parent != z))

    barrier = pltpu.get_barrier_semaphore()

    def greet(flag, device):
        @pl.when(flag)
        def _():
            pl.semaphore_signal(barrier, inc=1, device_id=device, device_id_type=MESH)

    greet(from_owner, (z, owner))
    greet(from_parent, (parent, c))
    greet(from_carrier, (z, carrier))

    def count(flag, amount=1):
        return jnp.where(flag, amount, 0)

    peers = (
        count(is_owner, jnp.where(z == owner_line, 1, 2))
        + count(up)
        + count(down)
        + count(extra_gives)
    )

    @pl.when(peers > 0)
    def _():
        pl.semaphore_wait(barrier, peers)

    def piece(q):
        return q // 4, (q // 2) % 2, pl.ds(pl.multiple_of((q % 2) * HALF, HALF), HALF)

    def src_copy(core, q):
        t, side, rows = piece(q)
        return remote(
            panel_ref.at[3 * core + t, side, rows],
            out_ref.at[t, side, rows],
            src_send.at[core, q],
            recv_sem.at[q],
            (z, 2 * z + core),
        )

    def lend_copy(q):
        t, side, rows = piece(q)
        return remote(
            panel_ref.at[3 * owner_core + t, side, rows],
            extra_ref.at[t, side, rows],
            src_send.at[owner_core, q],
            extra_recv.at[q],
            (z, carrier),
        )

    def chain_copy(ref, send, recv, device, q):
        t, side, rows = piece(q)
        here = ref.at[t, side, rows]
        return remote(here, here, send.at[q], recv.at[q], device)

    def give_copy(q):
        t, side, rows = piece(q)
        return remote(
            extra_ref.at[t, side, rows], out_ref.at[t, side, rows], give_send.at[q], recv_sem.at[q], (z, owner)
        )

    def up_copy(q):
        return chain_copy(out_ref, up_send, recv_sem, (first, c), q)

    def down_copy(q):
        return chain_copy(out_ref, down_send, recv_sem, (second, c), q)

    def extra_up_copy(q):
        return chain_copy(extra_ref, extra_up_send, extra_recv, (first, c), q)

    def extra_down_copy(q):
        return chain_copy(extra_ref, extra_down_send, extra_recv, (second, c), q)

    def loop(flag, body):
        @pl.when(flag)
        def _():
            lax.fori_loop(0, CHUNKS, lambda q, _: (body(q), 0)[1], 0)

    def when(flag, body):
        @pl.when(flag)
        def _():
            body()

    loop(holds_own, lambda q: lend_copy(q).start())
    for core in range(2):
        flag = is_owner if core != owner_core else sends_home
        loop(flag, lambda q, core=core: src_copy(core, q).start())

    @pl.when(holds_own)
    def _():
        copy = pltpu.make_async_copy(panel_ref.at[pl.ds(3 * owner_core, 3)], out_ref, local_sem)
        copy.start()
        copy.wait()

    def relay(q):
        when(receives, lambda: chain_copy(out_ref, up_send, recv_sem, (z, c + 1 - 2 * kind), q).wait_recv())
        when(up, lambda: up_copy(q).start())
        when(down, lambda: down_copy(q).start())

        @pl.when(extra_takes)
        def _():
            chain_copy(extra_ref, extra_up_send, extra_recv, (z, owner), q).wait_recv()
            when(extra_up, lambda: extra_up_copy(q).start())
            when(extra_down, lambda: extra_down_copy(q).start())
            when(extra_gives, lambda: give_copy(q).start())

    lax.fori_loop(0, CHUNKS, lambda q, _: (relay(q), 0)[1], 0)

    loop(holds_own, lambda q: lend_copy(q).wait_send())
    for core in range(2):
        flag = is_owner if core != owner_core else sends_home
        loop(flag, lambda q, core=core: src_copy(core, q).wait_send())
    loop(up, lambda q: up_copy(q).wait_send())
    loop(down, lambda q: down_copy(q).wait_send())
    loop(extra_up, lambda q: extra_up_copy(q).wait_send())
    loop(extra_down, lambda q: extra_down_copy(q).wait_send())
    loop(extra_gives, lambda q: give_copy(q).wait_send())


def spread_panel(owner, panel):
    return pl.pallas_call(
        functools.partial(panel_kernel, owner),
        out_shape=jax.ShapeDtypeStruct((3, 2, 96, 512), BF16),
        in_specs=[pl.BlockSpec(memory_space=pltpu.VMEM)],
        out_specs=pl.BlockSpec(memory_space=pltpu.VMEM),
        scratch_shapes=[
            pltpu.VMEM((3, 2, 96, 512), BF16),
            pltpu.SemaphoreType.DMA((2, CHUNKS)),
            pltpu.SemaphoreType.DMA((CHUNKS,)),
            pltpu.SemaphoreType.DMA((CHUNKS,)),
            pltpu.SemaphoreType.DMA((CHUNKS,)),
            pltpu.SemaphoreType.DMA((CHUNKS,)),
            pltpu.SemaphoreType.DMA((CHUNKS,)),
            pltpu.SemaphoreType.DMA((CHUNKS,)),
            pltpu.SemaphoreType.DMA((CHUNKS,)),
            pltpu.SemaphoreType.DMA,
        ],
        compiler_params=pltpu.CompilerParams(
            collective_id=owner - 15, has_side_effects=True, vmem_limit_bytes=16 * 2**20
        ),
        name="spread_panel",
    )(panel)


def dot_nt(a, b):
    return lax.dot_general(a, b, (((1,), (1,)), ((), ())), preferred_element_type=F32)


def dot_nn(a, b):
    return jnp.dot(a, b, preferred_element_type=F32)


def row_kernel(
    ranks_ref, step_ref, left_hbm, right_hbm, probe_hbm, upper_ref, sketch_ref, solve_ref, out_ref,
    left_ref, right_ref, probe_ref, stack_ref, reduced_ref,
    send_ref, got_ref, acc_ref, cur_ref, a_ref, b_ref, blk_ref,
    load_sem, send_sem, recv_sem, pair_send, pair_recv,
):
    z = lax.axis_index("row")
    c = lax.axis_index("col")
    x = c // 8
    y = (c // 2) % 4
    core = c % 2
    sibling = (z, c + 1 - 2 * core)

    def near(axis, by):
        beside = ((x + by) % 4) * 8 + y * 2 + core
        above = x * 8 + ((y + by) % 4) * 2 + core
        return (z, jnp.where(axis == 0, beside, above))

    def rows32(b):
        return pl.ds(pl.multiple_of(((b + 4) % 4) * 32, 32), 32)

    def cols(b):
        return pl.ds(pl.multiple_of(((b + 4) % 4) * 128, 128), 128)

    def spot(a):
        first = a % 2
        return first, 1 - first, jnp.where(first == 0, x, y), jnp.where(first == 0, y, x)

    def copies(a, n):
        first, second, u, v = spot(a)
        made = []
        for by in (1, 2, 3):
            if n == 0:
                src, dst = cur_ref.at[a, rows32(u + by)], a_ref.at[a, by - 1]
            elif n == 1:
                src, dst = cur_ref.at[a, rows32(u), cols(v + by)], b_ref.at[a, by - 1]
            elif n == 2:
                src = dst = blk_ref.at[a, :, cols(v)]
            else:
                src = dst = out_ref.at[core, a, rows32(u)]
            axis = first if n in (0, 3) else second
            sem = (a, n, by - 1)
            made.append(remote(src, dst, send_sem.at[sem], recv_sem.at[sem], near(axis, by)))
        return made

    def start(a, n):
        for copy in copies(a, n):
            copy.start()

    def arrive(a, n):
        first, second, u, v = spot(a)
        for by in (1, 2, 3):
            if n == 0:
                dst = a_ref.at[a, by - 1]
            elif n == 1:
                dst = b_ref.at[a, by - 1]
            elif n == 2:
                dst = blk_ref.at[a, :, cols(v - by)]
            else:
                dst = out_ref.at[core, a, rows32(u - by)]
            axis = first if n in (0, 3) else second
            sem = (a, n, by - 1)
            remote(dst, dst, send_sem.at[sem], recv_sem.at[sem], near(axis, by)).wait_recv()

    def pair_copy(a):
        return remote(send_ref.at[a], got_ref.at[a], pair_send.at[0, a], pair_recv.at[0, a], sibling)

    def give_copy(a, which):
        here = out_ref.at[which, a]
        return remote(here, here, pair_send.at[1, a], pair_recv.at[1, a], sibling)

    def loads(a):
        return [
            pltpu.make_async_copy(left_hbm.at[a], left_ref.at[a], load_sem.at[0, a]),
            pltpu.make_async_copy(right_hbm.at[a], right_ref.at[a], load_sem.at[1, a]),
            pltpu.make_async_copy(probe_hbm.at[a], probe_ref.at[a], load_sem.at[2, a]),
        ]

    def compute(a):
        column = step_ref[0]
        for copy in loads(a):
            copy.wait()
        level = lax.broadcasted_iota(jnp.int32, (128, 96), 1)
        live = z * 6 + a > column
        range_sum = jnp.zeros((128, 512), F32)
        co_sum = jnp.zeros((128, 512), F32)
        for j in range(3):
            tile = c * 3 + j
            own = tile == column
            depth = jnp.where(live & (tile <= column), ranks_ref[j, a], 0)
            keep = level < depth
            left = left_ref[a, j]
            right = right_ref[a, j]
            both = dot_nt(stack_ref[j], right)
            coupled = both[:96].astype(BF16)
            mixed = dot_nn(reduced_ref[j], coupled)
            mixed = jnp.where(own, -both[96:], mixed)
            mixed = jnp.where(keep, mixed, 0.0).astype(BF16)
            probed = dot_nt(probe_ref[a], left)
            probed = jnp.where(keep, probed, 0.0).astype(BF16)
            folded = dot_nt(probed, coupled).astype(BF16)
            folded = jnp.where(own, -probed, folded)
            closing = jnp.where(own, right, upper_ref[j, 1])
            range_sum += dot_nn(mixed, left)
            co_sum += dot_nn(folded, closing)
        even = core == 0
        acc_ref[a] = -jnp.where(even, range_sum, co_sum)
        send_ref[a] = -jnp.where(even, co_sum, range_sum).astype(BF16)
        pair_copy(a).start()

    def stage(n, a):
        first, second, u, v = spot(a)
        if n == 0:
            pair_copy(a).wait_recv()
            for by in range(4):
                rows = rows32(u + by)
                total = acc_ref[a, rows] + got_ref[a, rows].astype(F32)
                if by:
                    cur_ref[a, rows] = total.astype(BF16)
                else:
                    acc_ref[a, rows] = total
            start(a, 0)
        elif n == 1:
            arrive(a, 0)
            rows = rows32(u)
            total = acc_ref[a, rows]
            for d in range(3):
                total += a_ref[a, d].astype(F32)
            acc_ref[a, rows] = total
            cur_ref[a, rows] = total.astype(BF16)
            start(a, 1)
        elif n == 2:
            arrive(a, 1)
            total = acc_ref[a, rows32(u), cols(v)]
            for d in range(3):
                total += b_ref[a, d].astype(F32)
            blk_ref[a, :, cols(v)] = total.astype(BF16)
            start(a, 2)
        elif n == 3:
            arrive(a, 2)

            @pl.when(core == 0)
            def _():
                out_ref[0, a, rows32(u)] = blk_ref[a]

            @pl.when(core == 1)
            def _():
                out_ref[1, a, rows32(u)] = dot_nn(blk_ref[a], solve_ref[...]).astype(BF16)

            start(a, 3)
        elif n == 4:
            arrive(a, 3)
            give_copy(a, core).start()
        else:
            give_copy(a, 1 - core).wait_recv()

    @pl.when(z < FIRST)
    def _():
        out_ref[...] = jnp.zeros_like(out_ref)

    @pl.when(z >= FIRST)
    def _():
        for a in range(6):
            for copy in loads(a):
                copy.start()
        barrier = pltpu.get_barrier_semaphore()
        peers = (sibling, near(0, 1), near(0, 2), near(0, 3), near(1, 1), near(1, 2), near(1, 3))
        for device in peers:
            pl.semaphore_signal(barrier, inc=1, device_id=device, device_id_type=MESH)
        flat = sketch_ref[...].astype(F32).T.astype(BF16)
        for j in range(3):
            stack_ref[j, :96] = upper_ref[j, 0]
            stack_ref[j, 96:] = flat
            reduced = dot_nn(upper_ref[j, 1], sketch_ref[...]).astype(BF16).astype(F32)
            reduced_ref[j] = reduced.T.astype(BF16)
        pl.semaphore_wait(barrier, 7)

        def slot(t, _):
            @pl.when(t < 6)
            def _():
                compute(t)

            for n in reversed(range(6)):
                a = t - 1 - n

                @pl.when((a >= 0) & (a < 6))
                def _(n=n, a=a):
                    stage(n, a)

            return 0

        lax.fori_loop(0, 12, slot, 0)

        def finish(a, _):
            pair_copy(a).wait_send()
            give_copy(a, core).wait_send()
            for n in range(4):
                for copy in copies(a, n):
                    copy.wait_send()
            return 0

        lax.fori_loop(0, 6, finish, 0)


def row_sums(ranks, step, left, right, probes, upper, sketch, solve):
    vmem = pl.BlockSpec(memory_space=pltpu.VMEM)
    smem = pl.BlockSpec(memory_space=pltpu.SMEM)
    hbm = pl.BlockSpec(memory_space=pl.ANY)
    return pl.pallas_call(
        row_kernel,
        out_shape=jax.ShapeDtypeStruct((2, 6, 128, 512), BF16),
        in_specs=[smem, smem, hbm, hbm, hbm, vmem, vmem, vmem],
        out_specs=vmem,
        scratch_shapes=[
            pltpu.VMEM((6, 3, 96, 512), BF16),
            pltpu.VMEM((6, 3, 96, 512), BF16),
            pltpu.VMEM((6, 128, 512), BF16),
            pltpu.VMEM((3, 224, 512), BF16),
            pltpu.VMEM((3, 128, 96), BF16),
            pltpu.VMEM((6, 128, 512), BF16),
            pltpu.VMEM((6, 128, 512), BF16),
            pltpu.VMEM((6, 128, 512), F32),
            pltpu.VMEM((6, 128, 512), BF16),
            pltpu.VMEM((6, 3, 32, 512), BF16),
            pltpu.VMEM((6, 3, 32, 128), BF16),
            pltpu.VMEM((6, 32, 512), BF16),
            pltpu.SemaphoreType.DMA((3, 6)),
            pltpu.SemaphoreType.DMA((6, 4, 3)),
            pltpu.SemaphoreType.DMA((6, 4, 3)),
            pltpu.SemaphoreType.DMA((2, 6)),
            pltpu.SemaphoreType.DMA((2, 6)),
        ],
        compiler_params=pltpu.CompilerParams(
            collective_id=0, has_side_effects=True, vmem_limit_bytes=50 * 2**20
        ),
        name="row_sums",
    )(ranks, step, left, right, probes, upper, sketch, solve)


def body(left_factors, right_factors, ranks, sketch_left, sketch_right, upper_inverse, step):
    slots = ranks.T
    panel = gather_panel(slots, step, left_factors, right_factors)
    branches = [functools.partial(spread_panel, owner) for owner in range(16, 32)]
    upper = lax.switch(lax.div(step[0], 3) - 16, branches, panel)
    out = row_sums(
        slots, step, left_factors, right_factors, sketch_left, upper, sketch_right, upper_inverse
    )
    return (out[0], out[1])


def solution(mesh):
    return jax.shard_map(
        body,
        mesh=mesh,
        in_specs=(
            P("row", "col", None, None),
            P("row", "col", None, None),
            P("row", "col"),
            P("row", None, None),
            P(),
            P(),
            P(),
        ),
        out_specs=(P("row", None, None), P("row", None, None)),
        check_vma=False,
    )
```

```python
import functools

import jax
import jax.numpy as jnp
from jax import lax
from jax.experimental import pallas as pl
from jax.experimental.pallas import tpu as pltpu
from jax.sharding import PartitionSpec as P

MESH = pl.DeviceIdType.MESH
F32 = jnp.float32
BF16 = jnp.bfloat16
FIRST = 8
LAST = 15
HALF = 48
CHUNKS = 12


def remote(src, dst, send_sem, recv_sem, device):
    return pltpu.make_async_remote_copy(
        src_ref=src,
        dst_ref=dst,
        send_sem=send_sem,
        recv_sem=recv_sem,
        device_id=device,
        device_id_type=MESH,
    )


def line_trees():
    trees = []
    for s in range(16):
        parent = {}

        def chain(*planes):
            for before, after in zip(planes, planes[1:]):
                parent[after] = before

        low = s < FIRST
        if low or s == 15:
            chain(*((s, 4, 9) if s < 2 else (s, 5, 9) if s == 15 else (s, 9)), 10, 11)
            chain(9, 8)
        if low or s == 8:
            chain(*((s, 3, 14) if 6 <= s < 8 else (s, 2, 14) if s == 8 else (s, 14)), 13, 12)
            chain(14, 15)
        if s == 8:
            chain(8, 9, 10, 11)
        if s == 15:
            chain(15, 14, 13, 12)
        if s == 9:
            chain(9, 10, 11, 12, 13)
            chain(9, 8, 2, 15, 14)
        if s == 14:
            chain(14, 13, 12, 11, 10)
            chain(14, 15, 5, 8, 9)
        if 10 <= s <= 13:
            chain(*range(s, 16))
            chain(*range(s, 7, -1))
        trees.append(parent)
    return trees


def table_words(entries):
    return [
        sum(entries[s][4 * w + d] * 16**d for d in range(4)) for s in range(16) for w in range(4)
    ]


def tree_tables():
    none = [list(range(16)) for _ in range(16)]
    parents = [list(row) for row in none]
    firsts = [list(row) for row in none]
    seconds = [list(row) for row in none]
    for s, tree in enumerate(line_trees()):
        for plane, before in tree.items():
            parents[s][plane] = before
            if firsts[s][before] == before:
                firsts[s][before] = plane
            else:
                assert seconds[s][before] == before
                seconds[s][before] = plane
    return [table_words(entries) for entries in (parents, firsts, seconds)]


def look_up(words, s, z):
    index = s * 4 + z // 4
    word = words[0]
    for k, value in enumerate(words):
        if k:
            word = jnp.where(index == k, value, word)
    digit = z % 4
    scale = jnp.where(digit == 0, 1, jnp.where(digit == 1, 16, jnp.where(digit == 2, 256, 4096)))
    return (word // scale) % 16


def gather_kernel(ranks_ref, step_ref, left_ref, right_ref, panel_ref, sems):
    column = step_ref[0]
    slot = lax.rem(column, 3)

    @pl.when(lax.axis_index("col") == column // 3)
    def _():
        copies = [
            pltpu.make_async_copy(left_ref.at[:, slot], panel_ref.at[:, 0], sems.at[0]),
            pltpu.make_async_copy(right_ref.at[:, slot], panel_ref.at[:, 1], sems.at[1]),
        ]
        for copy in copies:
            copy.start()
        for copy in copies:
            copy.wait()
        level = lax.broadcasted_iota(jnp.int32, (96, 512), 0)
        for i in range(6):
            tile = panel_ref[i, 0]
            panel_ref[i, 0] = jnp.where(level < ranks_ref[slot, i], tile, jnp.zeros_like(tile))


def gather_panel(ranks, step, left, right):
    return pl.pallas_call(
        gather_kernel,
        out_shape=jax.ShapeDtypeStruct((6, 2, 96, 512), BF16),
        in_specs=[
            pl.BlockSpec(memory_space=pltpu.SMEM),
            pl.BlockSpec(memory_space=pltpu.SMEM),
            pl.BlockSpec(memory_space=pl.ANY),
            pl.BlockSpec(memory_space=pl.ANY),
        ],
        out_specs=pl.BlockSpec(memory_space=pltpu.VMEM),
        scratch_shapes=[pltpu.SemaphoreType.DMA((2,))],
        compiler_params=pltpu.CompilerParams(vmem_limit_bytes=62 * 2**20),
        name="gather_panel",
    )(ranks, step, left, right)


def panel_kernel(
    owner, panel_ref, out_ref, extra_ref, src_send, up_send, down_send, recv_sem,
    extra_up_send, extra_down_send, extra_recv, give_send, local_sem,
):
    z = lax.axis_index("row")
    c = lax.axis_index("col")
    s = c // 2
    kind = c % 2
    owner_line = owner // 2
    owner_core = owner % 2
    carrier = owner + 1 - 2 * owner_core
    home = z == s
    is_owner = c == owner
    is_carrier = c == carrier
    target = z >= FIRST
    parent, first, second = (look_up(words, s, z) for words in tree_tables())
    plain = jnp.logical_not(is_owner)
    up = plain & (first != z)
    down = plain & (second != z)
    from_owner = home & plain
    from_parent = plain & (parent != z)
    from_carrier = is_owner & target & (z != owner_line)
    receives = from_owner | from_parent | from_carrier
    sends_home = is_owner & (z != owner_line)
    holds_own = is_owner & (z == owner_line)
    extra_up = is_carrier & (first != z)
    extra_down = is_carrier & (second != z)
    extra_gives = is_carrier & target & (z != owner_line)
    extra_takes = is_carrier & (home | (parent != z))

    barrier = pltpu.get_barrier_semaphore()

    def greet(flag, device):
        @pl.when(flag)
        def _():
            pl.semaphore_signal(barrier, inc=1, device_id=device, device_id_type=MESH)

    greet(from_owner, (z, owner))
    greet(from_parent, (parent, c))
    greet(from_carrier, (z, carrier))

    def count(flag, amount=1):
        return jnp.where(flag, amount, 0)

    peers = (
        count(is_owner, jnp.where(z == owner_line, 1, 2))
        + count(up)
        + count(down)
        + count(extra_gives)
    )

    @pl.when(peers > 0)
    def _():
        pl.semaphore_wait(barrier, peers)

    def piece(q):
        return q // 4, (q // 2) % 2, pl.ds(pl.multiple_of((q % 2) * HALF, HALF), HALF)

    def src_copy(core, q):
        t, side, rows = piece(q)
        return remote(
            panel_ref.at[3 * core + t, side, rows],
            out_ref.at[t, side, rows],
            src_send.at[core, q],
            recv_sem.at[q],
            (z, 2 * z + core),
        )

    def lend_copy(q):
        t, side, rows = piece(q)
        return remote(
            panel_ref.at[3 * owner_core + t, side, rows],
            extra_ref.at[t, side, rows],
            src_send.at[owner_core, q],
            extra_recv.at[q],
            (z, carrier),
        )

    def chain_copy(ref, send, recv, device, q):
        t, side, rows = piece(q)
        here = ref.at[t, side, rows]
        return remote(here, here, send.at[q], recv.at[q], device)

    def give_copy(q):
        t, side, rows = piece(q)
        return remote(
            extra_ref.at[t, side, rows], out_ref.at[t, side, rows], give_send.at[q], recv_sem.at[q], (z, owner)
        )

    def up_copy(q):
        return chain_copy(out_ref, up_send, recv_sem, (first, c), q)

    def down_copy(q):
        return chain_copy(out_ref, down_send, recv_sem, (second, c), q)

    def extra_up_copy(q):
        return chain_copy(extra_ref, extra_up_send, extra_recv, (first, c), q)

    def extra_down_copy(q):
        return chain_copy(extra_ref, extra_down_send, extra_recv, (second, c), q)

    def loop(flag, body):
        @pl.when(flag)
        def _():
            lax.fori_loop(0, CHUNKS, lambda q, _: (body(q), 0)[1], 0)

    def when(flag, body):
        @pl.when(flag)
        def _():
            body()

    loop(holds_own, lambda q: lend_copy(q).start())
    for core in range(2):
        flag = is_owner if core != owner_core else sends_home
        loop(flag, lambda q, core=core: src_copy(core, q).start())

    @pl.when(holds_own)
    def _():
        copy = pltpu.make_async_copy(panel_ref.at[pl.ds(3 * owner_core, 3)], out_ref, local_sem)
        copy.start()
        copy.wait()

    def relay(q):
        when(receives, lambda: chain_copy(out_ref, up_send, recv_sem, (z, c + 1 - 2 * kind), q).wait_recv())
        when(up, lambda: up_copy(q).start())
        when(down, lambda: down_copy(q).start())

        @pl.when(extra_takes)
        def _():
            chain_copy(extra_ref, extra_up_send, extra_recv, (z, owner), q).wait_recv()
            when(extra_up, lambda: extra_up_copy(q).start())
            when(extra_down, lambda: extra_down_copy(q).start())
            when(extra_gives, lambda: give_copy(q).start())

    lax.fori_loop(0, CHUNKS, lambda q, _: (relay(q), 0)[1], 0)

    loop(holds_own, lambda q: lend_copy(q).wait_send())
    for core in range(2):
        flag = is_owner if core != owner_core else sends_home
        loop(flag, lambda q, core=core: src_copy(core, q).wait_send())
    loop(up, lambda q: up_copy(q).wait_send())
    loop(down, lambda q: down_copy(q).wait_send())
    loop(extra_up, lambda q: extra_up_copy(q).wait_send())
    loop(extra_down, lambda q: extra_down_copy(q).wait_send())
    loop(extra_gives, lambda q: give_copy(q).wait_send())


def spread_panel(owner, panel):
    return pl.pallas_call(
        functools.partial(panel_kernel, owner),
        out_shape=jax.ShapeDtypeStruct((3, 2, 96, 512), BF16),
        in_specs=[pl.BlockSpec(memory_space=pltpu.VMEM)],
        out_specs=pl.BlockSpec(memory_space=pltpu.VMEM),
        scratch_shapes=[
            pltpu.VMEM((3, 2, 96, 512), BF16),
            pltpu.SemaphoreType.DMA((2, CHUNKS)),
            pltpu.SemaphoreType.DMA((CHUNKS,)),
            pltpu.SemaphoreType.DMA((CHUNKS,)),
            pltpu.SemaphoreType.DMA((CHUNKS,)),
            pltpu.SemaphoreType.DMA((CHUNKS,)),
            pltpu.SemaphoreType.DMA((CHUNKS,)),
            pltpu.SemaphoreType.DMA((CHUNKS,)),
            pltpu.SemaphoreType.DMA((CHUNKS,)),
            pltpu.SemaphoreType.DMA,
        ],
        compiler_params=pltpu.CompilerParams(
            collective_id=owner - 15, has_side_effects=True, vmem_limit_bytes=16 * 2**20
        ),
        name="spread_panel",
    )(panel)


def dot_nt(a, b):
    return lax.dot_general(a, b, (((1,), (1,)), ((), ())), preferred_element_type=F32)


def dot_nn(a, b):
    return jnp.dot(a, b, preferred_element_type=F32)


GROUP = 2
GROUPS = 6 // GROUP


def row_kernel(
    ranks_ref, step_ref, left_hbm, right_hbm, probe_hbm, upper_ref, sketch_ref, solve_ref, out_ref,
    left_ref, right_ref, probe_ref, stack_ref, reduced_ref,
    send_ref, got_ref, acc_ref, cur_ref, a_ref, b_ref,
    load_sem, send_sem, recv_sem, pair_send, pair_recv,
):
    z = lax.axis_index("row")
    c = lax.axis_index("col")
    x = c // 8
    y = (c // 2) % 4
    core = c % 2
    even = core == 0
    sibling = (z, c + 1 - 2 * core)
    u = jnp.where(even, x, y)
    v = jnp.where(even, y, x)

    def along_x(by):
        return ((x + by) % 4) * 8 + y * 2 + core

    def along_y(by):
        return x * 8 + ((y + by) % 4) * 2 + core

    firsts = [(z, jnp.where(even, along_x(by), along_y(by))) for by in (1, 2, 3)]
    seconds = [(z, jnp.where(even, along_y(by), along_x(by))) for by in (1, 2, 3)]

    def rows32(b):
        return pl.ds(pl.multiple_of(((b + 4) % 4) * 32, 32), 32)

    def members(g):
        return pl.ds(g * GROUP, GROUP)

    def copies(g, n, landing):
        made = []
        for k in range(3):
            by = k + 1
            if n == 0:
                src, dst = cur_ref.at[members(g), rows32(u + by)], a_ref.at[g, k]
                if landing:
                    src = dst
            elif n == 1:
                src = dst = b_ref.at[g, (v - by + 4) % 4 if landing else v]
            else:
                src = dst = out_ref.at[core, members(g), rows32(u - by if landing else u)]
            device = seconds[k] if n == 1 else firsts[k]
            made.append(remote(src, dst, send_sem.at[g, n, k], recv_sem.at[g, n, k], device))
        return made

    def start(g, n):
        for copy in copies(g, n, False):
            copy.start()

    def arrive(g, n):
        for copy in copies(g, n, True):
            copy.wait_recv()

    def pair_copy(g):
        rows = members(g)
        return remote(send_ref.at[rows], got_ref.at[rows], pair_send.at[0, g], pair_recv.at[0, g], sibling)

    def give_copy(g, which):
        here = out_ref.at[which, members(g)]
        return remote(here, here, pair_send.at[1, g], pair_recv.at[1, g], sibling)

    def loads(g):
        rows = members(g)
        return [
            pltpu.make_async_copy(left_hbm.at[rows], left_ref.at[rows], load_sem.at[0, g]),
            pltpu.make_async_copy(right_hbm.at[rows], right_ref.at[rows], load_sem.at[1, g]),
            pltpu.make_async_copy(probe_hbm.at[rows], probe_ref.at[rows], load_sem.at[2, g]),
        ]

    def compute(g):
        column = step_ref[0]
        for copy in loads(g):
            copy.wait()
        level = lax.broadcasted_iota(jnp.int32, (128, 96), 1)
        tiles = [c * 3 + j for j in range(3)]
        both = [
            dot_nt(right_ref[members(g), j].reshape(GROUP * 96, 512), stack_ref[j]) for j in range(3)
        ]
        for k in range(GROUP):
            a = g * GROUP + k
            part = slice(96 * k, 96 * (k + 1))
            live = z * 6 + a > column
            own_reduced = jnp.where(
                tiles[0] == column,
                both[0][part, :128],
                jnp.where(tiles[1] == column, both[1][part, :128], both[2][part, :128]),
            )
            own_mixed = -own_reduced.T
            range_sum = jnp.zeros((128, 512), F32)
            co_sum = jnp.zeros((128, 512), F32)
            for j in range(3):
                own = tiles[j] == column
                depth = jnp.where(live & (tiles[j] <= column), ranks_ref[j, a], 0)
                keep = level < depth
                left = left_ref[a, j]
                coupled = both[j][part, 128:].astype(BF16)
                mixed = jnp.where(own, own_mixed, dot_nt(reduced_ref[j], coupled))
                mixed = jnp.where(keep, mixed, 0.0).astype(BF16)
                probed = dot_nt(probe_ref[a], left)
                probed = jnp.where(keep, probed, 0.0).astype(BF16)
                folded = dot_nn(probed, coupled).astype(BF16)
                folded = jnp.where(own, -probed, folded)
                closing = jnp.where(own, right_ref[a, j], upper_ref[j, 1])
                range_sum += dot_nn(mixed, left)
                co_sum += dot_nn(folded, closing)
            acc_ref[a] = -jnp.where(even, range_sum, co_sum)
            send_ref[a] = -jnp.where(even, co_sum, range_sum).astype(BF16)
        pair_copy(g).start()

    def stage(n, g):
        rows = members(g)
        if n == 0:
            pair_copy(g).wait_recv()
            for by in range(4):
                block = rows32(u + by)
                total = acc_ref[rows, block] + got_ref[rows, block].astype(F32)
                if by:
                    cur_ref[rows, block] = total.astype(BF16)
                else:
                    acc_ref[rows, block] = total
            start(g, 0)
        elif n == 1:
            arrive(g, 0)
            total = acc_ref[rows, rows32(u)]
            for k in range(3):
                total += a_ref[g, k].astype(F32)
            b_ref[g, v] = total.astype(BF16)
            start(g, 1)
        elif n == 2:
            arrive(g, 1)
            total = b_ref[g, 0].astype(F32)
            for b in range(1, 4):
                total += b_ref[g, b].astype(F32)
            block = total.astype(BF16)

            @pl.when(even)
            def _():
                out_ref[0, rows, rows32(u)] = block

            @pl.when(jnp.logical_not(even))
            def _():
                solved = dot_nn(block.reshape(GROUP * 32, 512), solve_ref[...]).astype(BF16)
                out_ref[1, rows, rows32(u)] = solved.reshape(GROUP, 32, 512)

            start(g, 2)
        elif n == 3:
            arrive(g, 2)
            give_copy(g, core).start()
        else:
            give_copy(g, 1 - core).wait_recv()

    @pl.when(z < FIRST)
    def _():
        out_ref[...] = jnp.zeros_like(out_ref)

    @pl.when(z >= FIRST)
    def _():
        for g in range(GROUPS):
            for copy in loads(g):
                copy.start()
        barrier = pltpu.get_barrier_semaphore()
        for device in (sibling, *firsts, *seconds):
            pl.semaphore_signal(barrier, inc=1, device_id=device, device_id_type=MESH)
        flat = sketch_ref[...].astype(F32).T.astype(BF16)
        for j in range(3):
            stack_ref[j, :128] = flat
            stack_ref[j, 128:] = upper_ref[j, 0]
            reduced = dot_nn(upper_ref[j, 1], sketch_ref[...]).astype(BF16).astype(F32)
            reduced_ref[j] = reduced.T.astype(BF16)
        pl.semaphore_wait(barrier, 7)

        def slot(t, _):
            @pl.when(t < GROUPS)
            def _():
                compute(t)

            for n in reversed(range(5)):
                g = t - 1 - n

                @pl.when((g >= 0) & (g < GROUPS))
                def _(n=n, g=g):
                    stage(n, g)

            return 0

        lax.fori_loop(0, GROUPS + 5, slot, 0)

        def finish(g, _):
            pair_copy(g).wait_send()
            give_copy(g, core).wait_send()
            for n in range(3):
                for copy in copies(g, n, False):
                    copy.wait_send()
            return 0

        lax.fori_loop(0, GROUPS, finish, 0)


def row_sums(ranks, step, left, right, probes, upper, sketch, solve):
    vmem = pl.BlockSpec(memory_space=pltpu.VMEM)
    smem = pl.BlockSpec(memory_space=pltpu.SMEM)
    hbm = pl.BlockSpec(memory_space=pl.ANY)
    return pl.pallas_call(
        row_kernel,
        out_shape=jax.ShapeDtypeStruct((2, 6, 128, 512), BF16),
        in_specs=[smem, smem, hbm, hbm, hbm, vmem, vmem, vmem],
        out_specs=vmem,
        scratch_shapes=[
            pltpu.VMEM((6, 3, 96, 512), BF16),
            pltpu.VMEM((6, 3, 96, 512), BF16),
            pltpu.VMEM((6, 128, 512), BF16),
            pltpu.VMEM((3, 224, 512), BF16),
            pltpu.VMEM((3, 128, 96), BF16),
            pltpu.VMEM((6, 128, 512), BF16),
            pltpu.VMEM((6, 128, 512), BF16),
            pltpu.VMEM((6, 128, 512), F32),
            pltpu.VMEM((6, 128, 512), BF16),
            pltpu.VMEM((GROUPS, 3, GROUP, 32, 512), BF16),
            pltpu.VMEM((GROUPS, 4, GROUP, 32, 512), BF16),
            pltpu.SemaphoreType.DMA((3, GROUPS)),
            pltpu.SemaphoreType.DMA((GROUPS, 3, 3)),
            pltpu.SemaphoreType.DMA((GROUPS, 3, 3)),
            pltpu.SemaphoreType.DMA((2, GROUPS)),
            pltpu.SemaphoreType.DMA((2, GROUPS)),
        ],
        compiler_params=pltpu.CompilerParams(
            collective_id=0, has_side_effects=True, vmem_limit_bytes=50 * 2**20
        ),
        name="row_sums",
    )(ranks, step, left, right, probes, upper, sketch, solve)


def body(left_factors, right_factors, ranks, sketch_left, sketch_right, upper_inverse, step):
    slots = ranks.T
    panel = gather_panel(slots, step, left_factors, right_factors)
    branches = [functools.partial(spread_panel, owner) for owner in range(16, 32)]
    upper = lax.switch(lax.div(step[0], 3) - 16, branches, panel)
    out = row_sums(
        slots, step, left_factors, right_factors, sketch_left, upper, sketch_right, upper_inverse
    )
    return (out[0], out[1])


def solution(mesh):
    return jax.shard_map(
        body,
        mesh=mesh,
        in_specs=(
            P("row", "col", None, None),
            P("row", "col", None, None),
            P("row", "col"),
            P("row", None, None),
            P(),
            P(),
            P(),
        ),
        out_specs=(P("row", None, None), P("row", None, None)),
        check_vma=False,
    )
```

```python
import functools

import jax
import jax.numpy as jnp
from jax import lax
from jax.experimental import pallas as pl
from jax.experimental.pallas import tpu as pltpu
from jax.sharding import PartitionSpec as P

MESH = pl.DeviceIdType.MESH
F32 = jnp.float32
BF16 = jnp.bfloat16
FIRST = 8
LAST = 15
HALF = 48
CHUNKS = 12


def remote(src, dst, send_sem, recv_sem, device):
    return pltpu.make_async_remote_copy(
        src_ref=src,
        dst_ref=dst,
        send_sem=send_sem,
        recv_sem=recv_sem,
        device_id=device,
        device_id_type=MESH,
    )


def line_trees():
    trees = []
    for s in range(16):
        parent = {}

        def chain(*planes):
            for before, after in zip(planes, planes[1:]):
                parent[after] = before

        low = s < FIRST
        if low or s == 15:
            chain(*((s, 4, 9) if s < 2 else (s, 5, 9) if s == 15 else (s, 9)), 10, 11)
            chain(9, 8)
        if low or s == 8:
            chain(*((s, 3, 14) if 6 <= s < 8 else (s, 2, 14) if s == 8 else (s, 14)), 13, 12)
            chain(14, 15)
        if s == 8:
            chain(8, 9, 10, 11)
        if s == 15:
            chain(15, 14, 13, 12)
        if s == 9:
            chain(9, 10, 11, 12, 13)
            chain(9, 8, 2, 15, 14)
        if s == 14:
            chain(14, 13, 12, 11, 10)
            chain(14, 15, 5, 8, 9)
        if 10 <= s <= 13:
            chain(*range(s, 16))
            chain(*range(s, 7, -1))
        trees.append(parent)
    return trees


def table_words(entries):
    return [
        sum(entries[s][4 * w + d] * 16**d for d in range(4)) for s in range(16) for w in range(4)
    ]


def tree_tables():
    none = [list(range(16)) for _ in range(16)]
    parents = [list(row) for row in none]
    firsts = [list(row) for row in none]
    seconds = [list(row) for row in none]
    for s, tree in enumerate(line_trees()):
        for plane, before in tree.items():
            parents[s][plane] = before
            if firsts[s][before] == before:
                firsts[s][before] = plane
            else:
                assert seconds[s][before] == before
                seconds[s][before] = plane
    return [table_words(entries) for entries in (parents, firsts, seconds)]


def look_up(words, s, z):
    index = s * 4 + z // 4
    word = words[0]
    for k, value in enumerate(words):
        if k:
            word = jnp.where(index == k, value, word)
    digit = z % 4
    scale = jnp.where(digit == 0, 1, jnp.where(digit == 1, 16, jnp.where(digit == 2, 256, 4096)))
    return (word // scale) % 16


def gather_kernel(ranks_ref, step_ref, left_ref, right_ref, panel_ref, sems):
    column = step_ref[0]
    slot = lax.rem(column, 3)

    @pl.when(lax.axis_index("col") == column // 3)
    def _():
        copies = [
            pltpu.make_async_copy(left_ref.at[:, slot], panel_ref.at[:, 0], sems.at[0]),
            pltpu.make_async_copy(right_ref.at[:, slot], panel_ref.at[:, 1], sems.at[1]),
        ]
        for copy in copies:
            copy.start()
        for copy in copies:
            copy.wait()
        level = lax.broadcasted_iota(jnp.int32, (96, 512), 0)
        for i in range(6):
            tile = panel_ref[i, 0]
            panel_ref[i, 0] = jnp.where(level < ranks_ref[slot, i], tile, jnp.zeros_like(tile))


def gather_panel(ranks, step, left, right):
    return pl.pallas_call(
        gather_kernel,
        out_shape=jax.ShapeDtypeStruct((6, 2, 96, 512), BF16),
        in_specs=[
            pl.BlockSpec(memory_space=pltpu.SMEM),
            pl.BlockSpec(memory_space=pltpu.SMEM),
            pl.BlockSpec(memory_space=pl.ANY),
            pl.BlockSpec(memory_space=pl.ANY),
        ],
        out_specs=pl.BlockSpec(memory_space=pltpu.VMEM),
        scratch_shapes=[pltpu.SemaphoreType.DMA((2,))],
        compiler_params=pltpu.CompilerParams(vmem_limit_bytes=62 * 2**20),
        name="gather_panel",
    )(ranks, step, left, right)


def home_kernel(owner, panel_ref, out_ref, send_sem, recv_sem, local_sem):
    z = lax.axis_index("row")
    c = lax.axis_index("col")
    owner_line = owner // 2
    owner_core = owner % 2
    is_owner = c == owner
    is_home = (c // 2 == z) & jnp.logical_not(is_owner)
    holds_own = is_owner & (z == owner_line)
    barrier = pltpu.get_barrier_semaphore()

    @pl.when(is_home)
    def _():
        pl.semaphore_signal(barrier, inc=1, device_id=(z, owner), device_id_type=MESH)

    def copy(core):
        part = panel_ref.at[pl.ds(3 * core, 3)]
        return remote(part, out_ref, send_sem.at[core], recv_sem, (z, 2 * z + core))

    @pl.when(is_owner)
    def _():
        pl.semaphore_wait(barrier, jnp.where(z == owner_line, 1, 2))

    for core in range(2):
        flag = is_owner if core != owner_core else is_owner & (z != owner_line)

        @pl.when(flag)
        def _(core=core):
            copy(core).start()

    @pl.when(holds_own)
    def _():
        own = pltpu.make_async_copy(panel_ref.at[pl.ds(3 * owner_core, 3)], out_ref, local_sem)
        own.start()
        own.wait()

    @pl.when(is_home)
    def _():
        remote(out_ref, out_ref, send_sem.at[0], recv_sem, (z, owner)).wait_recv()

    for core in range(2):
        flag = is_owner if core != owner_core else is_owner & (z != owner_line)

        @pl.when(flag)
        def _(core=core):
            copy(core).wait_send()


def send_home(owner, panel):
    return pl.pallas_call(
        functools.partial(home_kernel, owner),
        out_shape=jax.ShapeDtypeStruct((3, 2, 96, 512), BF16),
        in_specs=[pl.BlockSpec(memory_space=pltpu.VMEM)],
        out_specs=pl.BlockSpec(memory_space=pltpu.VMEM),
        scratch_shapes=[
            pltpu.SemaphoreType.DMA((2,)),
            pltpu.SemaphoreType.DMA,
            pltpu.SemaphoreType.DMA,
        ],
        compiler_params=pltpu.CompilerParams(
            collective_id=owner - 15, has_side_effects=True, vmem_limit_bytes=16 * 2**20
        ),
        name="send_home",
    )(panel)


def dot_nt(a, b):
    return lax.dot_general(a, b, (((1,), (1,)), ((), ())), preferred_element_type=F32)


def dot_nn(a, b):
    return jnp.dot(a, b, preferred_element_type=F32)


GROUP = 2
GROUPS = 6 // GROUP


def row_kernel(
    ranks_ref, step_ref, left_hbm, right_hbm, probe_hbm, home_ref, sketch_ref, solve_ref, out_ref,
    upper_ref, left_ref, right_ref, probe_ref, probed_ref, stack_ref, reduced_ref,
    range_ref, co_ref, send_ref, got_ref, acc_ref, cur_ref, a_ref, b_ref,
    home_sem, up_send, down_send, chunk_sem, load_sem, send_sem, recv_sem, pair_send, pair_recv,
):
    z = lax.axis_index("row")
    c = lax.axis_index("col")
    x = c // 8
    y = (c // 2) % 4
    core = c % 2
    even = core == 0
    sibling = (z, c + 1 - 2 * core)
    u = jnp.where(even, x, y)
    v = jnp.where(even, y, x)

    def along_x(by):
        return ((x + by) % 4) * 8 + y * 2 + core

    def along_y(by):
        return x * 8 + ((y + by) % 4) * 2 + core

    firsts = [(z, jnp.where(even, along_x(by), along_y(by))) for by in (1, 2, 3)]
    seconds = [(z, jnp.where(even, along_y(by), along_x(by))) for by in (1, 2, 3)]

    def rows32(b):
        return pl.ds(pl.multiple_of(((b + 4) % 4) * 32, 32), 32)

    def members(g):
        return pl.ds(g * GROUP, GROUP)

    def copies(g, n, landing):
        made = []
        for k in range(3):
            by = k + 1
            if n == 0:
                src, dst = cur_ref.at[members(g), rows32(u + by)], a_ref.at[g, k]
                if landing:
                    src = dst
            elif n == 1:
                src = dst = b_ref.at[g, (v - by + 4) % 4 if landing else v]
            else:
                src = dst = out_ref.at[core, members(g), rows32(u - by if landing else u)]
            device = seconds[k] if n == 1 else firsts[k]
            made.append(remote(src, dst, send_sem.at[g, n, k], recv_sem.at[g, n, k], device))
        return made

    def start(g, n):
        for copy in copies(g, n, False):
            copy.start()

    def arrive(g, n):
        for copy in copies(g, n, True):
            copy.wait_recv()

    def pair_copy(g):
        rows = members(g)
        return remote(send_ref.at[rows], got_ref.at[rows], pair_send.at[0, g], pair_recv.at[0, g], sibling)

    def give_copy(g, which):
        here = out_ref.at[which, members(g)]
        return remote(here, here, pair_send.at[1, g], pair_recv.at[1, g], sibling)

    def loads(g):
        rows = members(g)
        return [
            pltpu.make_async_copy(left_hbm.at[rows], left_ref.at[rows], load_sem.at[0, g]),
            pltpu.make_async_copy(right_hbm.at[rows], right_ref.at[rows], load_sem.at[1, g]),
            pltpu.make_async_copy(probe_hbm.at[rows], probe_ref.at[rows], load_sem.at[2, g]),
        ]

    line = c // 2
    home = z == line
    target = z >= FIRST
    parent, first, second = (look_up(words, line, z) for words in tree_tables())
    receives = parent != z
    up = first != z
    down = second != z

    def piece(q):
        return q // 4, (q // 2) % 2, pl.ds(pl.multiple_of((q % 2) * HALF, HALF), HALF)

    def chunk_copy(ref, sems, plane, q):
        t, side, rows = piece(q)
        return remote(
            ref.at[t, side, rows], upper_ref.at[t, side, rows], sems.at[q], chunk_sem.at[q], (plane, c)
        )

    def forward(ref, q):
        @pl.when(up)
        def _():
            chunk_copy(ref, up_send, first, q).start()

        @pl.when(down)
        def _():
            chunk_copy(ref, down_send, second, q).start()

    def relay(q):
        @pl.when(receives)
        def _():
            chunk_copy(upper_ref, up_send, parent, q).wait_recv()
            forward(upper_ref, q)

    def keep_of(a, t):
        tile = c * 3 + t
        live = z * 6 + a > step_ref[0]
        depth = jnp.where(live & (tile <= step_ref[0]), ranks_ref[t, a], 0)
        return lax.broadcasted_iota(jnp.int32, (128, 96), 1) < depth

    def probes(g, _):
        for copy in loads(g):
            copy.wait()
        for k in range(GROUP):
            a = g * GROUP + k
            range_ref[a] = jnp.zeros((128, 512), F32)
            co_ref[a] = jnp.zeros((128, 512), F32)
            for t in range(3):
                probed = dot_nt(probe_ref[a], left_ref[a, t])
                probed_ref[a, t] = jnp.where(keep_of(a, t), probed, 0.0).astype(BF16)
        return 0

    def open_tile(t):
        stack_ref[128:] = upper_ref[t, 0]
        reduced = dot_nn(upper_ref[t, 1], sketch_ref[...]).astype(BF16).astype(F32)
        reduced_ref[...] = reduced.T.astype(BF16)

    def compute(t, g):
        own = c * 3 + t == step_ref[0]
        both = dot_nt(right_ref[members(g), t].reshape(GROUP * 96, 512), stack_ref[...])
        for k in range(GROUP):
            a = g * GROUP + k
            part = slice(96 * k, 96 * (k + 1))
            coupled = both[part, 128:].astype(BF16)
            mixed = jnp.where(own, -both[part, :128].T, dot_nt(reduced_ref[...], coupled))
            mixed = jnp.where(keep_of(a, t), mixed, 0.0).astype(BF16)
            probed = probed_ref[a, t]
            folded = jnp.where(own, -probed, dot_nn(probed, coupled).astype(BF16))
            closing = jnp.where(own, right_ref[a, t], upper_ref[t, 1])
            range_ref[a] += dot_nn(mixed, left_ref[a, t])
            co_ref[a] += dot_nn(folded, closing)

            @pl.when((t < 2) & (g < 2))
            def _(k=k):
                relay(t * 4 + 4 + g * 2 + k)

    def close_rows(g):
        for k in range(GROUP):
            a = g * GROUP + k
            acc_ref[a] = -jnp.where(even, range_ref[a], co_ref[a])
            send_ref[a] = -jnp.where(even, co_ref[a], range_ref[a]).astype(BF16)
        pair_copy(g).start()

    def stage(n, g):
        rows = members(g)
        if n == 0:
            pair_copy(g).wait_recv()
            for by in range(4):
                block = rows32(u + by)
                total = acc_ref[rows, block] + got_ref[rows, block].astype(F32)
                if by:
                    cur_ref[rows, block] = total.astype(BF16)
                else:
                    acc_ref[rows, block] = total
            start(g, 0)
        elif n == 1:
            arrive(g, 0)
            total = acc_ref[rows, rows32(u)]
            for k in range(3):
                total += a_ref[g, k].astype(F32)
            b_ref[g, v] = total.astype(BF16)
            start(g, 1)
        elif n == 2:
            arrive(g, 1)
            total = b_ref[g, 0].astype(F32)
            for b in range(1, 4):
                total += b_ref[g, b].astype(F32)
            block = total.astype(BF16)

            @pl.when(even)
            def _():
                out_ref[0, rows, rows32(u)] = block

            @pl.when(jnp.logical_not(even))
            def _():
                solved = dot_nn(block.reshape(GROUP * 32, 512), solve_ref[...]).astype(BF16)
                out_ref[1, rows, rows32(u)] = solved.reshape(GROUP, 32, 512)

            start(g, 2)
        elif n == 3:
            arrive(g, 2)
            give_copy(g, core).start()
        else:
            give_copy(g, 1 - core).wait_recv()

    @pl.when(target)
    def _():
        for g in range(GROUPS):
            for copy in loads(g):
                copy.start()

    barrier = pltpu.get_barrier_semaphore()

    @pl.when(receives)
    def _():
        pl.semaphore_signal(barrier, inc=1, device_id=(parent, c), device_id_type=MESH)

    @pl.when(target)
    def _():
        for device in (sibling, *firsts, *seconds):
            pl.semaphore_signal(barrier, inc=1, device_id=device, device_id_type=MESH)

    peers = jnp.where(up, 1, 0) + jnp.where(down, 1, 0) + jnp.where(target, 7, 0)

    @pl.when(peers > 0)
    def _():
        pl.semaphore_wait(barrier, peers)

    @pl.when(home)
    def _():
        own = pltpu.make_async_copy(home_ref, upper_ref, home_sem)
        own.start()
        lax.fori_loop(0, CHUNKS, lambda q, _: (forward(home_ref, q), 0)[1], 0)
        own.wait()

    @pl.when(jnp.logical_not(target))
    def _():
        out_ref[...] = jnp.zeros_like(out_ref)
        lax.fori_loop(0, CHUNKS, lambda q, _: (relay(q), 0)[1], 0)

    @pl.when(target)
    def _():
        stack_ref[:128] = sketch_ref[...].astype(F32).T.astype(BF16)
        lax.fori_loop(0, GROUPS, probes, 0)
        lax.fori_loop(0, 4, lambda q, _: (relay(q), 0)[1], 0)

        def step(i, _):
            t = i // GROUPS
            g = i % GROUPS

            @pl.when(t < 3)
            def _():
                @pl.when(g == 0)
                def _():
                    open_tile(t)

                compute(t, g)

            @pl.when(t == 2)
            def _():
                close_rows(g)

            for n in reversed(range(5)):
                late = i - 2 * GROUPS - 1 - n

                @pl.when((late >= 0) & (late < GROUPS))
                def _(n=n, late=late):
                    stage(n, late)

            return 0

        lax.fori_loop(0, 3 * GROUPS + 5, step, 0)

        def finish(g, _):
            pair_copy(g).wait_send()
            give_copy(g, core).wait_send()
            for n in range(3):
                for copy in copies(g, n, False):
                    copy.wait_send()
            return 0

        lax.fori_loop(0, GROUPS, finish, 0)

    @pl.when(up)
    def _():
        lax.fori_loop(
            0, CHUNKS, lambda q, _: (chunk_copy(upper_ref, up_send, first, q).wait_send(), 0)[1], 0
        )

    @pl.when(down)
    def _():
        lax.fori_loop(
            0, CHUNKS, lambda q, _: (chunk_copy(upper_ref, down_send, second, q).wait_send(), 0)[1], 0
        )


def row_sums(ranks, step, left, right, probes, home, sketch, solve):
    vmem = pl.BlockSpec(memory_space=pltpu.VMEM)
    smem = pl.BlockSpec(memory_space=pltpu.SMEM)
    hbm = pl.BlockSpec(memory_space=pl.ANY)
    return pl.pallas_call(
        row_kernel,
        out_shape=jax.ShapeDtypeStruct((2, 6, 128, 512), BF16),
        in_specs=[smem, smem, hbm, hbm, hbm, vmem, vmem, vmem],
        out_specs=vmem,
        scratch_shapes=[
            pltpu.VMEM((3, 2, 96, 512), BF16),
            pltpu.VMEM((6, 3, 96, 512), BF16),
            pltpu.VMEM((6, 3, 96, 512), BF16),
            pltpu.VMEM((6, 128, 512), BF16),
            pltpu.VMEM((6, 3, 128, 96), BF16),
            pltpu.VMEM((224, 512), BF16),
            pltpu.VMEM((128, 96), BF16),
            pltpu.VMEM((6, 128, 512), F32),
            pltpu.VMEM((6, 128, 512), F32),
            pltpu.VMEM((6, 128, 512), BF16),
            pltpu.VMEM((6, 128, 512), BF16),
            pltpu.VMEM((6, 128, 512), F32),
            pltpu.VMEM((6, 128, 512), BF16),
            pltpu.VMEM((GROUPS, 3, GROUP, 32, 512), BF16),
            pltpu.VMEM((GROUPS, 4, GROUP, 32, 512), BF16),
            pltpu.SemaphoreType.DMA,
            pltpu.SemaphoreType.DMA((CHUNKS,)),
            pltpu.SemaphoreType.DMA((CHUNKS,)),
            pltpu.SemaphoreType.DMA((CHUNKS,)),
            pltpu.SemaphoreType.DMA((3, GROUPS)),
            pltpu.SemaphoreType.DMA((GROUPS, 3, 3)),
            pltpu.SemaphoreType.DMA((GROUPS, 3, 3)),
            pltpu.SemaphoreType.DMA((2, GROUPS)),
            pltpu.SemaphoreType.DMA((2, GROUPS)),
        ],
        compiler_params=pltpu.CompilerParams(
            collective_id=0, has_side_effects=True, vmem_limit_bytes=50 * 2**20
        ),
        name="row_sums",
    )(ranks, step, left, right, probes, home, sketch, solve)


def body(left_factors, right_factors, ranks, sketch_left, sketch_right, upper_inverse, step):
    slots = ranks.T
    panel = gather_panel(slots, step, left_factors, right_factors)
    branches = [functools.partial(send_home, owner) for owner in range(16, 32)]
    home = lax.switch(lax.div(step[0], 3) - 16, branches, panel)
    out = row_sums(
        slots, step, left_factors, right_factors, sketch_left, home, sketch_right, upper_inverse
    )
    return (out[0], out[1])


def solution(mesh):
    return jax.shard_map(
        body,
        mesh=mesh,
        in_specs=(
            P("row", "col", None, None),
            P("row", "col", None, None),
            P("row", "col"),
            P("row", None, None),
            P(),
            P(),
            P(),
        ),
        out_specs=(P("row", None, None), P("row", None, None)),
        check_vma=False,
    )
```

```python
import functools

import jax
import jax.numpy as jnp
from jax import lax
from jax.experimental import pallas as pl
from jax.experimental.pallas import tpu as pltpu
from jax.sharding import PartitionSpec as P

MESH = pl.DeviceIdType.MESH
F32 = jnp.float32
BF16 = jnp.bfloat16
FIRST = 8
LAST = 15
HALF = 48
CHUNKS = 12


def remote(src, dst, send_sem, recv_sem, device):
    return pltpu.make_async_remote_copy(
        src_ref=src,
        dst_ref=dst,
        send_sem=send_sem,
        recv_sem=recv_sem,
        device_id=device,
        device_id_type=MESH,
    )


def line_trees():
    trees = []
    for s in range(16):
        parent = {}

        def chain(*planes):
            for before, after in zip(planes, planes[1:]):
                parent[after] = before

        low = s < FIRST
        if low or s == 15:
            chain(*((s, 4, 9) if s < 2 else (s, 5, 9) if s == 15 else (s, 9)), 10, 11)
            chain(9, 8)
        if low or s == 8:
            chain(*((s, 3, 14) if 6 <= s < 8 else (s, 2, 14) if s == 8 else (s, 14)), 13, 12)
            chain(14, 15)
        if s == 8:
            chain(8, 9, 10, 11)
        if s == 15:
            chain(15, 14, 13, 12)
        if s == 9:
            chain(9, 10, 11, 12, 13)
            chain(9, 8, 2, 15, 14)
        if s == 14:
            chain(14, 13, 12, 11, 10)
            chain(14, 15, 5, 8, 9)
        if 10 <= s <= 13:
            chain(*range(s, 16))
            chain(*range(s, 7, -1))
        trees.append(parent)
    return trees


def table_words(entries):
    return [
        sum(entries[s][4 * w + d] * 16**d for d in range(4)) for s in range(16) for w in range(4)
    ]


def tree_tables():
    none = [list(range(16)) for _ in range(16)]
    parents = [list(row) for row in none]
    firsts = [list(row) for row in none]
    seconds = [list(row) for row in none]
    for s, tree in enumerate(line_trees()):
        for plane, before in tree.items():
            parents[s][plane] = before
            if firsts[s][before] == before:
                firsts[s][before] = plane
            else:
                assert seconds[s][before] == before
                seconds[s][before] = plane
    return [table_words(entries) for entries in (parents, firsts, seconds)]


def look_up(words, s, z):
    index = s * 4 + z // 4
    word = words[0]
    for k, value in enumerate(words):
        if k:
            word = jnp.where(index == k, value, word)
    digit = z % 4
    scale = jnp.where(digit == 0, 1, jnp.where(digit == 1, 16, jnp.where(digit == 2, 256, 4096)))
    return (word // scale) % 16


def gather_kernel(ranks_ref, step_ref, left_ref, right_ref, panel_ref, sems):
    column = step_ref[0]
    slot = lax.rem(column, 3)

    @pl.when(lax.axis_index("col") == column // 3)
    def _():
        copies = [
            pltpu.make_async_copy(left_ref.at[:, slot], panel_ref.at[:, 0], sems.at[0]),
            pltpu.make_async_copy(right_ref.at[:, slot], panel_ref.at[:, 1], sems.at[1]),
        ]
        for copy in copies:
            copy.start()
        for copy in copies:
            copy.wait()
        level = lax.broadcasted_iota(jnp.int32, (96, 512), 0)
        for i in range(6):
            tile = panel_ref[i, 0]
            panel_ref[i, 0] = jnp.where(level < ranks_ref[slot, i], tile, jnp.zeros_like(tile))


def gather_panel(ranks, step, left, right):
    return pl.pallas_call(
        gather_kernel,
        out_shape=jax.ShapeDtypeStruct((6, 2, 96, 512), BF16),
        in_specs=[
            pl.BlockSpec(memory_space=pltpu.SMEM),
            pl.BlockSpec(memory_space=pltpu.SMEM),
            pl.BlockSpec(memory_space=pl.ANY),
            pl.BlockSpec(memory_space=pl.ANY),
        ],
        out_specs=pl.BlockSpec(memory_space=pltpu.VMEM),
        scratch_shapes=[pltpu.SemaphoreType.DMA((2,))],
        compiler_params=pltpu.CompilerParams(vmem_limit_bytes=62 * 2**20),
        name="gather_panel",
    )(ranks, step, left, right)


def dot_nt(a, b):
    return lax.dot_general(a, b, (((1,), (1,)), ((), ())), preferred_element_type=F32)


def dot_nn(a, b):
    return jnp.dot(a, b, preferred_element_type=F32)


GROUP = 2
GROUPS = 6 // GROUP


def row_kernel(
    owner, ranks_ref, step_ref, left_hbm, right_hbm, probe_hbm, panel_ref, sketch_ref, solve_ref, out_ref,
    upper_ref, extra_ref, left_ref, right_ref, probe_ref, probed_ref, stack_ref, reduced_ref,
    range_ref, co_ref, send_ref, got_ref, acc_ref, cur_ref, a_ref, b_ref,
    src_send, up_send, down_send, chunk_sem, extra_up_send, extra_down_send, extra_recv, give_send,
    local_sem, load_sem, send_sem, recv_sem, pair_send, pair_recv,
):
    z = lax.axis_index("row")
    c = lax.axis_index("col")
    x = c // 8
    y = (c // 2) % 4
    core = c % 2
    even = core == 0
    sibling = (z, c + 1 - 2 * core)
    u = jnp.where(even, x, y)
    v = jnp.where(even, y, x)

    def along_x(by):
        return ((x + by) % 4) * 8 + y * 2 + core

    def along_y(by):
        return x * 8 + ((y + by) % 4) * 2 + core

    firsts = [(z, jnp.where(even, along_x(by), along_y(by))) for by in (1, 2, 3)]
    seconds = [(z, jnp.where(even, along_y(by), along_x(by))) for by in (1, 2, 3)]

    def rows32(b):
        return pl.ds(pl.multiple_of(((b + 4) % 4) * 32, 32), 32)

    def members(g):
        return pl.ds(g * GROUP, GROUP)

    def copies(g, n, landing):
        made = []
        for k in range(3):
            by = k + 1
            if n == 0:
                src, dst = cur_ref.at[members(g), rows32(u + by)], a_ref.at[g, k]
                if landing:
                    src = dst
            elif n == 1:
                src = dst = b_ref.at[g, (v - by + 4) % 4 if landing else v]
            else:
                src = dst = out_ref.at[core, members(g), rows32(u - by if landing else u)]
            device = seconds[k] if n == 1 else firsts[k]
            made.append(remote(src, dst, send_sem.at[g, n, k], recv_sem.at[g, n, k], device))
        return made

    def start(g, n):
        for copy in copies(g, n, False):
            copy.start()

    def arrive(g, n):
        for copy in copies(g, n, True):
            copy.wait_recv()

    def pair_copy(g):
        rows = members(g)
        return remote(send_ref.at[rows], got_ref.at[rows], pair_send.at[0, g], pair_recv.at[0, g], sibling)

    def give_copy(g, which):
        here = out_ref.at[which, members(g)]
        return remote(here, here, pair_send.at[1, g], pair_recv.at[1, g], sibling)

    def loads(g):
        rows = members(g)
        return [
            pltpu.make_async_copy(left_hbm.at[rows], left_ref.at[rows], load_sem.at[0, g]),
            pltpu.make_async_copy(right_hbm.at[rows], right_ref.at[rows], load_sem.at[1, g]),
            pltpu.make_async_copy(probe_hbm.at[rows], probe_ref.at[rows], load_sem.at[2, g]),
        ]

    s = c // 2
    kind = c % 2
    owner_line = owner // 2
    owner_core = owner % 2
    carrier = owner + 1 - 2 * owner_core
    home = z == s
    is_owner = c == owner
    is_carrier = c == carrier
    target = z >= FIRST
    parent, first, second = (look_up(words, s, z) for words in tree_tables())
    plain = jnp.logical_not(is_owner)
    up = plain & (first != z)
    down = plain & (second != z)
    from_owner = home & plain
    from_parent = plain & (parent != z)
    from_carrier = is_owner & target & (z != owner_line)
    receives = from_owner | from_parent | from_carrier
    sends_home = is_owner & (z != owner_line)
    holds_own = is_owner & (z == owner_line)
    extra_up = is_carrier & (first != z)
    extra_down = is_carrier & (second != z)
    extra_gives = is_carrier & target & (z != owner_line)
    extra_takes = is_carrier & (home | (parent != z))

    def piece(q):
        return q // 4, (q // 2) % 2, pl.ds(pl.multiple_of((q % 2) * HALF, HALF), HALF)

    def src_copy(core, q):
        t, side, rows = piece(q)
        return remote(
            panel_ref.at[3 * core + t, side, rows],
            upper_ref.at[t, side, rows],
            src_send.at[core, q],
            chunk_sem.at[q],
            (z, 2 * z + core),
        )

    def lend_copy(q):
        t, side, rows = piece(q)
        return remote(
            panel_ref.at[3 * owner_core + t, side, rows],
            extra_ref.at[t, side, rows],
            src_send.at[owner_core, q],
            extra_recv.at[q],
            (z, carrier),
        )

    def chain_copy(ref, send, recv, device, q):
        t, side, rows = piece(q)
        here = ref.at[t, side, rows]
        return remote(here, here, send.at[q], recv.at[q], device)

    def hand_copy(q):
        t, side, rows = piece(q)
        return remote(
            extra_ref.at[t, side, rows], upper_ref.at[t, side, rows], give_send.at[q], chunk_sem.at[q], (z, owner)
        )

    def up_copy(q):
        return chain_copy(upper_ref, up_send, chunk_sem, (first, c), q)

    def down_copy(q):
        return chain_copy(upper_ref, down_send, chunk_sem, (second, c), q)

    def extra_up_copy(q):
        return chain_copy(extra_ref, extra_up_send, extra_recv, (first, c), q)

    def extra_down_copy(q):
        return chain_copy(extra_ref, extra_down_send, extra_recv, (second, c), q)

    def loop(flag, body):
        @pl.when(flag)
        def _():
            lax.fori_loop(0, CHUNKS, lambda q, _: (body(q), 0)[1], 0)

    def when(flag, body):
        @pl.when(flag)
        def _():
            body()

    def relay(q):
        when(receives, lambda: chain_copy(upper_ref, up_send, chunk_sem, (z, c + 1 - 2 * kind), q).wait_recv())
        when(up, lambda: up_copy(q).start())
        when(down, lambda: down_copy(q).start())

        @pl.when(extra_takes)
        def _():
            chain_copy(extra_ref, extra_up_send, extra_recv, (z, owner), q).wait_recv()
            when(extra_up, lambda: extra_up_copy(q).start())
            when(extra_down, lambda: extra_down_copy(q).start())
            when(extra_gives, lambda: hand_copy(q).start())

    def keep_of(a, t):
        tile = c * 3 + t
        live = z * 6 + a > step_ref[0]
        depth = jnp.where(live & (tile <= step_ref[0]), ranks_ref[t, a], 0)
        return lax.broadcasted_iota(jnp.int32, (128, 96), 1) < depth

    def probes(g, _):
        for copy in loads(g):
            copy.wait()
        for k in range(GROUP):
            a = g * GROUP + k
            range_ref[a] = jnp.zeros((128, 512), F32)
            co_ref[a] = jnp.zeros((128, 512), F32)
            for t in range(3):
                probed = dot_nt(probe_ref[a], left_ref[a, t])
                probed_ref[a, t] = jnp.where(keep_of(a, t), probed, 0.0).astype(BF16)
        return 0

    def open_tile(t):
        stack_ref[128:] = upper_ref[t, 0]
        reduced = dot_nn(upper_ref[t, 1], sketch_ref[...]).astype(BF16).astype(F32)
        reduced_ref[...] = reduced.T.astype(BF16)

    def compute(t, g):
        own = c * 3 + t == step_ref[0]
        both = dot_nt(right_ref[members(g), t].reshape(GROUP * 96, 512), stack_ref[...])
        for k in range(GROUP):
            a = g * GROUP + k
            part = slice(96 * k, 96 * (k + 1))
            coupled = both[part, 128:].astype(BF16)
            mixed = jnp.where(own, -both[part, :128].T, dot_nt(reduced_ref[...], coupled))
            mixed = jnp.where(keep_of(a, t), mixed, 0.0).astype(BF16)
            probed = probed_ref[a, t]
            folded = jnp.where(own, -probed, dot_nn(probed, coupled).astype(BF16))
            closing = jnp.where(own, right_ref[a, t], upper_ref[t, 1])
            range_ref[a] += dot_nn(mixed, left_ref[a, t])
            co_ref[a] += dot_nn(folded, closing)

            q = 4 + t * 6 + g * GROUP + k

            @pl.when(q < CHUNKS)
            def _(q=q):
                relay(q)

    def close_rows(g):
        for k in range(GROUP):
            a = g * GROUP + k
            acc_ref[a] = -jnp.where(even, range_ref[a], co_ref[a])
            send_ref[a] = -jnp.where(even, co_ref[a], range_ref[a]).astype(BF16)
        pair_copy(g).start()

    def stage(n, g):
        rows = members(g)
        if n == 0:
            pair_copy(g).wait_recv()
            for by in range(4):
                block = rows32(u + by)
                total = acc_ref[rows, block] + got_ref[rows, block].astype(F32)
                if by:
                    cur_ref[rows, block] = total.astype(BF16)
                else:
                    acc_ref[rows, block] = total
            start(g, 0)
        elif n == 1:
            arrive(g, 0)
            total = acc_ref[rows, rows32(u)]
            for k in range(3):
                total += a_ref[g, k].astype(F32)
            b_ref[g, v] = total.astype(BF16)
            start(g, 1)
        elif n == 2:
            arrive(g, 1)
            total = b_ref[g, 0].astype(F32)
            for b in range(1, 4):
                total += b_ref[g, b].astype(F32)
            block = total.astype(BF16)

            @pl.when(even)
            def _():
                out_ref[0, rows, rows32(u)] = block

            @pl.when(jnp.logical_not(even))
            def _():
                solved = dot_nn(block.reshape(GROUP * 32, 512), solve_ref[...]).astype(BF16)
                out_ref[1, rows, rows32(u)] = solved.reshape(GROUP, 32, 512)

            start(g, 2)
        elif n == 3:
            arrive(g, 2)
            give_copy(g, core).start()
        else:
            give_copy(g, 1 - core).wait_recv()

    @pl.when(target)
    def _():
        for g in range(GROUPS):
            for copy in loads(g):
                copy.start()

    barrier = pltpu.get_barrier_semaphore()

    def greet(flag, device):
        @pl.when(flag)
        def _():
            pl.semaphore_signal(barrier, inc=1, device_id=device, device_id_type=MESH)

    greet(from_owner, (z, owner))
    greet(from_parent, (parent, c))
    greet(from_carrier, (z, carrier))

    @pl.when(target)
    def _():
        for device in (sibling, *firsts, *seconds):
            pl.semaphore_signal(barrier, inc=1, device_id=device, device_id_type=MESH)

    def count(flag, amount=1):
        return jnp.where(flag, amount, 0)

    peers = (
        count(is_owner, jnp.where(z == owner_line, 1, 2))
        + count(up)
        + count(down)
        + count(extra_gives)
        + count(target, 7)
    )

    @pl.when(peers > 0)
    def _():
        pl.semaphore_wait(barrier, peers)

    loop(holds_own, lambda q: lend_copy(q).start())
    for half in range(2):
        flag = is_owner if half != owner_core else sends_home
        loop(flag, lambda q, half=half: src_copy(half, q).start())

    @pl.when(holds_own)
    def _():
        copy = pltpu.make_async_copy(panel_ref.at[pl.ds(3 * owner_core, 3)], upper_ref, local_sem)
        copy.start()
        copy.wait()

    @pl.when(jnp.logical_not(target))
    def _():
        out_ref[...] = jnp.zeros_like(out_ref)

    loop(jnp.logical_not(target), relay)

    @pl.when(target)
    def _():
        stack_ref[:128] = sketch_ref[...].astype(F32).T.astype(BF16)
        lax.fori_loop(0, GROUPS, probes, 0)
        lax.fori_loop(0, 4, lambda q, _: (relay(q), 0)[1], 0)

        def step(i, _):
            t = i // GROUPS
            g = i % GROUPS

            @pl.when(t < 3)
            def _():
                @pl.when(g == 0)
                def _():
                    open_tile(t)

                compute(t, g)

            @pl.when(t == 2)
            def _():
                close_rows(g)

            for n in reversed(range(5)):
                late = i - 2 * GROUPS - 1 - n

                @pl.when((late >= 0) & (late < GROUPS))
                def _(n=n, late=late):
                    stage(n, late)

            return 0

        lax.fori_loop(0, 3 * GROUPS + 5, step, 0)

        def finish(g, _):
            pair_copy(g).wait_send()
            give_copy(g, core).wait_send()
            for n in range(3):
                for copy in copies(g, n, False):
                    copy.wait_send()
            return 0

        lax.fori_loop(0, GROUPS, finish, 0)

    loop(holds_own, lambda q: lend_copy(q).wait_send())
    for half in range(2):
        flag = is_owner if half != owner_core else sends_home
        loop(flag, lambda q, half=half: src_copy(half, q).wait_send())
    loop(up, lambda q: up_copy(q).wait_send())
    loop(down, lambda q: down_copy(q).wait_send())
    loop(extra_up, lambda q: extra_up_copy(q).wait_send())
    loop(extra_down, lambda q: extra_down_copy(q).wait_send())
    loop(extra_gives, lambda q: hand_copy(q).wait_send())


def row_sums(owner, ranks, step, left, right, probes, panel, sketch, solve):
    vmem = pl.BlockSpec(memory_space=pltpu.VMEM)
    smem = pl.BlockSpec(memory_space=pltpu.SMEM)
    hbm = pl.BlockSpec(memory_space=pl.ANY)
    return pl.pallas_call(
        functools.partial(row_kernel, owner),
        out_shape=jax.ShapeDtypeStruct((2, 6, 128, 512), BF16),
        in_specs=[smem, smem, hbm, hbm, hbm, vmem, vmem, vmem],
        out_specs=vmem,
        scratch_shapes=[
            pltpu.VMEM((3, 2, 96, 512), BF16),
            pltpu.VMEM((3, 2, 96, 512), BF16),
            pltpu.VMEM((6, 3, 96, 512), BF16),
            pltpu.VMEM((6, 3, 96, 512), BF16),
            pltpu.VMEM((6, 128, 512), BF16),
            pltpu.VMEM((6, 3, 128, 96), BF16),
            pltpu.VMEM((224, 512), BF16),
            pltpu.VMEM((128, 96), BF16),
            pltpu.VMEM((6, 128, 512), F32),
            pltpu.VMEM((6, 128, 512), F32),
            pltpu.VMEM((6, 128, 512), BF16),
            pltpu.VMEM((6, 128, 512), BF16),
            pltpu.VMEM((6, 128, 512), F32),
            pltpu.VMEM((6, 128, 512), BF16),
            pltpu.VMEM((GROUPS, 3, GROUP, 32, 512), BF16),
            pltpu.VMEM((GROUPS, 4, GROUP, 32, 512), BF16),
            pltpu.SemaphoreType.DMA((2, CHUNKS)),
            *[pltpu.SemaphoreType.DMA((CHUNKS,))] * 7,
            pltpu.SemaphoreType.DMA,
            pltpu.SemaphoreType.DMA((3, GROUPS)),
            pltpu.SemaphoreType.DMA((GROUPS, 3, 3)),
            pltpu.SemaphoreType.DMA((GROUPS, 3, 3)),
            pltpu.SemaphoreType.DMA((2, GROUPS)),
            pltpu.SemaphoreType.DMA((2, GROUPS)),
        ],
        compiler_params=pltpu.CompilerParams(
            collective_id=owner - 16, has_side_effects=True, vmem_limit_bytes=50 * 2**20
        ),
        name="row_sums",
    )(ranks, step, left, right, probes, panel, sketch, solve)


def body(left_factors, right_factors, ranks, sketch_left, sketch_right, upper_inverse, step):
    slots = ranks.T
    panel = gather_panel(slots, step, left_factors, right_factors)
    branches = [functools.partial(row_sums, owner) for owner in range(16, 32)]
    out = lax.switch(
        lax.div(step[0], 3) - 16, branches, slots, step, left_factors, right_factors, sketch_left,
        panel, sketch_right, upper_inverse,
    )
    return (out[0], out[1])


def solution(mesh):
    return jax.shard_map(
        body,
        mesh=mesh,
        in_specs=(
            P("row", "col", None, None),
            P("row", "col", None, None),
            P("row", "col"),
            P("row", None, None),
            P(),
            P(),
            P(),
        ),
        out_specs=(P("row", None, None), P("row", None, None)),
        check_vma=False,
    )
```

```python
import functools

import jax
import jax.numpy as jnp
from jax import lax
from jax.experimental import pallas as pl
from jax.experimental.pallas import tpu as pltpu
from jax.sharding import PartitionSpec as P

MESH = pl.DeviceIdType.MESH
F32 = jnp.float32
BF16 = jnp.bfloat16
FIRST = 8
LAST = 15
PIECE = 32
CHUNKS = 18


def remote(src, dst, send_sem, recv_sem, device):
    return pltpu.make_async_remote_copy(
        src_ref=src,
        dst_ref=dst,
        send_sem=send_sem,
        recv_sem=recv_sem,
        device_id=device,
        device_id_type=MESH,
    )


def line_trees():
    paths = {
        0: [(0, 4, 9, 8), (9, 10), (0, 14, 15), (14, 13, 12, 11)],
        1: [(1, 8, 9, 10), (1, 14, 15), (14, 13, 12, 11)],
        2: [(2, 8, 9, 10), (2, 14, 15), (14, 13, 12, 11)],
        3: [(3, 9, 8), (9, 10, 11), (3, 14, 15), (14, 13, 12)],
        4: [(4, 9, 8), (9, 10, 11), (4, 14, 15), (14, 13, 12)],
        5: [(5, 9, 8), (9, 10, 11, 12), (5, 15, 14, 13)],
        6: [(6, 9, 8), (9, 10, 11, 12), (6, 15, 14, 13)],
        7: [(7, 9, 8), (9, 10, 11, 12), (7, 3, 14, 15), (14, 13)],
        8: [(8, 9, 10, 11, 12, 13), (8, 2, 15, 14)],
        9: [(9, 10, 11, 12, 13, 14), (9, 8, 2, 15)],
        10: [(10, 11, 12, 13, 14, 15), (10, 9, 8)],
        11: [(11, 12, 13, 14, 15), (11, 10, 9, 8)],
        12: [(12, 13, 14, 15), (12, 11, 10, 9, 8)],
        13: [(13, 14, 15), (13, 12, 11, 10, 9, 8)],
        14: [(14, 13, 12, 11, 10, 9), (14, 15, 5, 8)],
        15: [(15, 14, 13, 12, 11, 10), (15, 5, 8, 9)],
    }
    trees = []
    for s in range(16):
        parent = {}
        for path in paths[s]:
            for before, after in zip(path, path[1:]):
                assert after not in parent and after != s
                parent[after] = before
        trees.append(parent)
    return trees


def table_words(entries):
    return [
        sum(entries[s][4 * w + d] * 16**d for d in range(4)) for s in range(16) for w in range(4)
    ]


def tree_tables():
    none = [list(range(16)) for _ in range(16)]
    parents = [list(row) for row in none]
    firsts = [list(row) for row in none]
    seconds = [list(row) for row in none]
    for s, tree in enumerate(line_trees()):
        for plane, before in tree.items():
            parents[s][plane] = before
            if firsts[s][before] == before:
                firsts[s][before] = plane
            else:
                assert seconds[s][before] == before
                seconds[s][before] = plane
    return [table_words(entries) for entries in (parents, firsts, seconds)]


def look_up(words, s, z):
    index = s * 4 + z // 4
    word = words[0]
    for k, value in enumerate(words):
        if k:
            word = jnp.where(index == k, value, word)
    digit = z % 4
    scale = jnp.where(digit == 0, 1, jnp.where(digit == 1, 16, jnp.where(digit == 2, 256, 4096)))
    return (word // scale) % 16


def gather_kernel(ranks_ref, step_ref, left_ref, right_ref, panel_ref, sems):
    column = step_ref[0]
    slot = lax.rem(column, 3)

    @pl.when(lax.axis_index("col") == column // 3)
    def _():
        copies = [
            pltpu.make_async_copy(left_ref.at[:, slot], panel_ref.at[:, 0], sems.at[0]),
            pltpu.make_async_copy(right_ref.at[:, slot], panel_ref.at[:, 1], sems.at[1]),
        ]
        for copy in copies:
            copy.start()
        for copy in copies:
            copy.wait()
        level = lax.broadcasted_iota(jnp.int32, (96, 512), 0)
        for i in range(6):
            tile = panel_ref[i, 0]
            panel_ref[i, 0] = jnp.where(level < ranks_ref[slot, i], tile, jnp.zeros_like(tile))


def gather_panel(ranks, step, left, right):
    return pl.pallas_call(
        gather_kernel,
        out_shape=jax.ShapeDtypeStruct((6, 2, 96, 512), BF16),
        in_specs=[
            pl.BlockSpec(memory_space=pltpu.SMEM),
            pl.BlockSpec(memory_space=pltpu.SMEM),
            pl.BlockSpec(memory_space=pl.ANY),
            pl.BlockSpec(memory_space=pl.ANY),
        ],
        out_specs=pl.BlockSpec(memory_space=pltpu.VMEM),
        scratch_shapes=[pltpu.SemaphoreType.DMA((2,))],
        compiler_params=pltpu.CompilerParams(vmem_limit_bytes=62 * 2**20),
        name="gather_panel",
    )(ranks, step, left, right)


def panel_kernel(
    owner, panel_ref, out_ref, extra_ref, src_send, up_send, down_send, recv_sem,
    extra_up_send, extra_down_send, extra_recv, give_send, local_sem,
):
    z = lax.axis_index("row")
    c = lax.axis_index("col")
    s = c // 2
    kind = c % 2
    owner_line = owner // 2
    owner_core = owner % 2
    carrier = owner + 1 - 2 * owner_core
    home = z == s
    is_owner = c == owner
    is_carrier = c == carrier
    target = z >= FIRST
    parent, first, second = (look_up(words, s, z) for words in tree_tables())
    plain = jnp.logical_not(is_owner)
    up = plain & (first != z)
    down = plain & (second != z)
    from_owner = home & plain
    from_parent = plain & (parent != z)
    from_carrier = is_owner & target & (z != owner_line)
    receives = from_owner | from_parent | from_carrier
    sends_home = is_owner & (z != owner_line)
    holds_own = is_owner & (z == owner_line)
    extra_up = is_carrier & (first != z)
    extra_down = is_carrier & (second != z)
    extra_gives = is_carrier & target & (z != owner_line)
    extra_takes = is_carrier & (home | (parent != z))

    barrier = pltpu.get_barrier_semaphore()

    def greet(flag, device):
        @pl.when(flag)
        def _():
            pl.semaphore_signal(barrier, inc=1, device_id=device, device_id_type=MESH)

    greet(from_owner, (z, owner))
    greet(from_parent, (parent, c))
    greet(from_carrier, (z, carrier))

    def count(flag, amount=1):
        return jnp.where(flag, amount, 0)

    peers = (
        count(is_owner, jnp.where(z == owner_line, 1, 2))
        + count(up)
        + count(down)
        + count(extra_gives)
    )

    @pl.when(peers > 0)
    def _():
        pl.semaphore_wait(barrier, peers)

    def piece(q):
        return q // 6, (q // 3) % 2, pl.ds(pl.multiple_of((q % 3) * PIECE, PIECE), PIECE)

    def src_copy(core, q):
        t, side, rows = piece(q)
        return remote(
            panel_ref.at[3 * core + t, side, rows],
            out_ref.at[t, side, rows],
            src_send.at[core, q],
            recv_sem.at[q],
            (z, 2 * z + core),
        )

    def lend_copy(q):
        t, side, rows = piece(q)
        return remote(
            panel_ref.at[3 * owner_core + t, side, rows],
            extra_ref.at[t, side, rows],
            src_send.at[owner_core, q],
            extra_recv.at[q],
            (z, carrier),
        )

    def chain_copy(ref, send, recv, device, q):
        t, side, rows = piece(q)
        here = ref.at[t, side, rows]
        return remote(here, here, send.at[q], recv.at[q], device)

    def give_copy(q):
        t, side, rows = piece(q)
        return remote(
            extra_ref.at[t, side, rows], out_ref.at[t, side, rows], give_send.at[q], recv_sem.at[q], (z, owner)
        )

    def up_copy(q):
        return chain_copy(out_ref, up_send, recv_sem, (first, c), q)

    def down_copy(q):
        return chain_copy(out_ref, down_send, recv_sem, (second, c), q)

    def extra_up_copy(q):
        return chain_copy(extra_ref, extra_up_send, extra_recv, (first, c), q)

    def extra_down_copy(q):
        return chain_copy(extra_ref, extra_down_send, extra_recv, (second, c), q)

    def loop(flag, body):
        @pl.when(flag)
        def _():
            lax.fori_loop(0, CHUNKS, lambda q, _: (body(q), 0)[1], 0)

    def when(flag, body):
        @pl.when(flag)
        def _():
            body()

    loop(holds_own, lambda q: lend_copy(q).start())
    for core in range(2):
        flag = is_owner if core != owner_core else sends_home
        loop(flag, lambda q, core=core: src_copy(core, q).start())

    @pl.when(holds_own)
    def _():
        copy = pltpu.make_async_copy(panel_ref.at[pl.ds(3 * owner_core, 3)], out_ref, local_sem)
        copy.start()
        copy.wait()

    def relay(q):
        when(receives, lambda: chain_copy(out_ref, up_send, recv_sem, (z, c + 1 - 2 * kind), q).wait_recv())
        when(up, lambda: up_copy(q).start())
        when(down, lambda: down_copy(q).start())

        @pl.when(extra_takes)
        def _():
            chain_copy(extra_ref, extra_up_send, extra_recv, (z, owner), q).wait_recv()
            when(extra_up, lambda: extra_up_copy(q).start())
            when(extra_down, lambda: extra_down_copy(q).start())
            when(extra_gives, lambda: give_copy(q).start())

    lax.fori_loop(0, CHUNKS, lambda q, _: (relay(q), 0)[1], 0)

    loop(holds_own, lambda q: lend_copy(q).wait_send())
    for core in range(2):
        flag = is_owner if core != owner_core else sends_home
        loop(flag, lambda q, core=core: src_copy(core, q).wait_send())
    loop(up, lambda q: up_copy(q).wait_send())
    loop(down, lambda q: down_copy(q).wait_send())
    loop(extra_up, lambda q: extra_up_copy(q).wait_send())
    loop(extra_down, lambda q: extra_down_copy(q).wait_send())
    loop(extra_gives, lambda q: give_copy(q).wait_send())


def spread_panel(owner, panel):
    return pl.pallas_call(
        functools.partial(panel_kernel, owner),
        out_shape=jax.ShapeDtypeStruct((3, 2, 96, 512), BF16),
        in_specs=[pl.BlockSpec(memory_space=pltpu.VMEM)],
        out_specs=pl.BlockSpec(memory_space=pltpu.VMEM),
        scratch_shapes=[
            pltpu.VMEM((3, 2, 96, 512), BF16),
            pltpu.SemaphoreType.DMA((2, CHUNKS)),
            pltpu.SemaphoreType.DMA((CHUNKS,)),
            pltpu.SemaphoreType.DMA((CHUNKS,)),
            pltpu.SemaphoreType.DMA((CHUNKS,)),
            pltpu.SemaphoreType.DMA((CHUNKS,)),
            pltpu.SemaphoreType.DMA((CHUNKS,)),
            pltpu.SemaphoreType.DMA((CHUNKS,)),
            pltpu.SemaphoreType.DMA((CHUNKS,)),
            pltpu.SemaphoreType.DMA,
        ],
        compiler_params=pltpu.CompilerParams(
            collective_id=owner - 15, has_side_effects=True, vmem_limit_bytes=16 * 2**20
        ),
        name="spread_panel",
    )(panel)


def dot_nt(a, b):
    return lax.dot_general(a, b, (((1,), (1,)), ((), ())), preferred_element_type=F32)


def dot_nn(a, b):
    return jnp.dot(a, b, preferred_element_type=F32)


GROUP = 2
GROUPS = 6 // GROUP


def row_kernel(
    ranks_ref, step_ref, left_hbm, right_hbm, probe_hbm, upper_ref, sketch_ref, solve_ref, out_ref,
    left_ref, right_ref, probe_ref, reduced_ref,
    send_ref, got_ref, acc_ref, cur_ref, a_ref, b_ref,
    load_sem, send_sem, recv_sem, pair_send, pair_recv,
):
    z = lax.axis_index("row")
    c = lax.axis_index("col")
    x = c // 8
    y = (c // 2) % 4
    core = c % 2
    even = core == 0
    sibling = (z, c + 1 - 2 * core)
    u = jnp.where(even, x, y)
    v = jnp.where(even, y, x)

    def along_x(by):
        return ((x + by) % 4) * 8 + y * 2 + core

    def along_y(by):
        return x * 8 + ((y + by) % 4) * 2 + core

    firsts = [(z, jnp.where(even, along_x(by), along_y(by))) for by in (1, 2, 3)]
    seconds = [(z, jnp.where(even, along_y(by), along_x(by))) for by in (1, 2, 3)]

    def rows32(b):
        return pl.ds(pl.multiple_of(((b + 4) % 4) * 32, 32), 32)

    def members(g):
        return pl.ds(g * GROUP, GROUP)

    def copies(g, n, landing):
        made = []
        for k in range(3):
            by = k + 1
            if n == 0:
                src, dst = cur_ref.at[members(g), rows32(u + by)], a_ref.at[g, k]
                if landing:
                    src = dst
            elif n == 1:
                src = dst = b_ref.at[g, (v - by + 4) % 4 if landing else v]
            else:
                src = dst = out_ref.at[core, members(g), rows32(u - by if landing else u)]
            device = seconds[k] if n == 1 else firsts[k]
            made.append(remote(src, dst, send_sem.at[g, n, k], recv_sem.at[g, n, k], device))
        return made

    def start(g, n):
        for copy in copies(g, n, False):
            copy.start()

    def arrive(g, n):
        for copy in copies(g, n, True):
            copy.wait_recv()

    def pair_copy(g):
        rows = members(g)
        return remote(send_ref.at[rows], got_ref.at[rows], pair_send.at[0, g], pair_recv.at[0, g], sibling)

    def give_copy(g, which):
        here = out_ref.at[which, members(g)]
        return remote(here, here, pair_send.at[1, g], pair_recv.at[1, g], sibling)

    def loads(g):
        rows = members(g)
        return [
            pltpu.make_async_copy(left_hbm.at[rows], left_ref.at[rows], load_sem.at[0, g]),
            pltpu.make_async_copy(right_hbm.at[rows], right_ref.at[rows], load_sem.at[1, g]),
            pltpu.make_async_copy(probe_hbm.at[rows], probe_ref.at[rows], load_sem.at[2, g]),
        ]

    def compute(g):
        column = step_ref[0]
        for copy in loads(g):
            copy.wait()
        level = lax.broadcasted_iota(jnp.int32, (128, 96), 1)
        tiles = [c * 3 + j for j in range(3)]
        both = [
            dot_nt(right_ref[members(g), j].reshape(GROUP * 96, 512), upper_ref[j, 0]) for j in range(3)
        ]
        for k in range(GROUP):
            a = g * GROUP + k
            part = slice(96 * k, 96 * (k + 1))
            live = z * 6 + a > column
            own_right = jnp.where(
                tiles[0] == column,
                right_ref[a, 0],
                jnp.where(tiles[1] == column, right_ref[a, 1], right_ref[a, 2]),
            )
            own_mixed = -dot_nn(own_right, sketch_ref[...]).T
            range_sum = jnp.zeros((128, 512), F32)
            co_sum = jnp.zeros((128, 512), F32)
            for j in range(3):
                own = tiles[j] == column
                depth = jnp.where(live & (tiles[j] <= column), ranks_ref[j, a], 0)
                keep = level < depth
                left = left_ref[a, j]
                coupled = both[j][part].astype(BF16)
                mixed = jnp.where(own, own_mixed, dot_nt(reduced_ref[j], coupled))
                mixed = jnp.where(keep, mixed, 0.0).astype(BF16)
                probed = dot_nt(probe_ref[a], left)
                probed = jnp.where(keep, probed, 0.0).astype(BF16)
                folded = dot_nn(probed, coupled).astype(BF16)
                folded = jnp.where(own, -probed, folded)
                closing = jnp.where(own, own_right, upper_ref[j, 1])
                range_sum += dot_nn(mixed, left)
                co_sum += dot_nn(folded, closing)
            acc_ref[a] = -jnp.where(even, range_sum, co_sum)
            send_ref[a] = -jnp.where(even, co_sum, range_sum).astype(BF16)
        pair_copy(g).start()

    def stage(n, g):
        rows = members(g)
        if n == 0:
            pair_copy(g).wait_recv()
            for by in range(4):
                block = rows32(u + by)
                total = acc_ref[rows, block] + got_ref[rows, block].astype(F32)
                if by:
                    cur_ref[rows, block] = total.astype(BF16)
                else:
                    acc_ref[rows, block] = total
            start(g, 0)
        elif n == 1:
            arrive(g, 0)
            total = acc_ref[rows, rows32(u)]
            for k in range(3):
                total += a_ref[g, k].astype(F32)
            b_ref[g, v] = total.astype(BF16)
            start(g, 1)
        elif n == 2:
            arrive(g, 1)
            total = b_ref[g, 0].astype(F32)
            for b in range(1, 4):
                total += b_ref[g, b].astype(F32)
            block = total.astype(BF16)

            @pl.when(even)
            def _():
                out_ref[0, rows, rows32(u)] = block

            @pl.when(jnp.logical_not(even))
            def _():
                solved = dot_nn(block.reshape(GROUP * 32, 512), solve_ref[...]).astype(BF16)
                out_ref[1, rows, rows32(u)] = solved.reshape(GROUP, 32, 512)

            start(g, 2)
        elif n == 3:
            arrive(g, 2)
            give_copy(g, core).start()
        else:
            give_copy(g, 1 - core).wait_recv()

    @pl.when(z < FIRST)
    def _():
        out_ref[...] = jnp.zeros_like(out_ref)

    @pl.when(z >= FIRST)
    def _():
        for g in range(GROUPS):
            for copy in loads(g):
                copy.start()
        barrier = pltpu.get_barrier_semaphore()
        for device in (sibling, *firsts, *seconds):
            pl.semaphore_signal(barrier, inc=1, device_id=device, device_id_type=MESH)
        for j in range(3):
            reduced = dot_nn(upper_ref[j, 1], sketch_ref[...]).astype(BF16).astype(F32)
            reduced_ref[j] = reduced.T.astype(BF16)
        pl.semaphore_wait(barrier, 7)

        def slot(t, _):
            @pl.when(t < GROUPS)
            def _():
                compute(t)

            for n in reversed(range(5)):
                g = t - 1 - n

                @pl.when((g >= 0) & (g < GROUPS))
                def _(n=n, g=g):
                    stage(n, g)

            return 0

        lax.fori_loop(0, GROUPS + 5, slot, 0)

        def finish(g, _):
            pair_copy(g).wait_send()
            give_copy(g, core).wait_send()
            for n in range(3):
                for copy in copies(g, n, False):
                    copy.wait_send()
            return 0

        lax.fori_loop(0, GROUPS, finish, 0)


def row_sums(ranks, step, left, right, probes, upper, sketch, solve):
    vmem = pl.BlockSpec(memory_space=pltpu.VMEM)
    smem = pl.BlockSpec(memory_space=pltpu.SMEM)
    hbm = pl.BlockSpec(memory_space=pl.ANY)
    return pl.pallas_call(
        row_kernel,
        out_shape=jax.ShapeDtypeStruct((2, 6, 128, 512), BF16),
        in_specs=[smem, smem, hbm, hbm, hbm, vmem, vmem, vmem],
        out_specs=vmem,
        scratch_shapes=[
            pltpu.VMEM((6, 3, 96, 512), BF16),
            pltpu.VMEM((6, 3, 96, 512), BF16),
            pltpu.VMEM((6, 128, 512), BF16),
            pltpu.VMEM((3, 128, 96), BF16),
            pltpu.VMEM((6, 128, 512), BF16),
            pltpu.VMEM((6, 128, 512), BF16),
            pltpu.VMEM((6, 128, 512), F32),
            pltpu.VMEM((6, 128, 512), BF16),
            pltpu.VMEM((GROUPS, 3, GROUP, 32, 512), BF16),
            pltpu.VMEM((GROUPS, 4, GROUP, 32, 512), BF16),
            pltpu.SemaphoreType.DMA((3, GROUPS)),
            pltpu.SemaphoreType.DMA((GROUPS, 3, 3)),
            pltpu.SemaphoreType.DMA((GROUPS, 3, 3)),
            pltpu.SemaphoreType.DMA((2, GROUPS)),
            pltpu.SemaphoreType.DMA((2, GROUPS)),
        ],
        compiler_params=pltpu.CompilerParams(
            collective_id=0, has_side_effects=True, vmem_limit_bytes=50 * 2**20
        ),
        name="row_sums",
    )(ranks, step, left, right, probes, upper, sketch, solve)


def body(left_factors, right_factors, ranks, sketch_left, sketch_right, upper_inverse, step):
    slots = ranks.T
    panel = gather_panel(slots, step, left_factors, right_factors)
    branches = [functools.partial(spread_panel, owner) for owner in range(16, 32)]
    upper = lax.switch(lax.div(step[0], 3) - 16, branches, panel)
    out = row_sums(
        slots, step, left_factors, right_factors, sketch_left, upper, sketch_right, upper_inverse
    )
    return (out[0], out[1])


def solution(mesh):
    return jax.shard_map(
        body,
        mesh=mesh,
        in_specs=(
            P("row", "col", None, None),
            P("row", "col", None, None),
            P("row", "col"),
            P("row", None, None),
            P(),
            P(),
            P(),
        ),
        out_specs=(P("row", None, None), P("row", None, None)),
        check_vma=False,
    )
```

```python
import functools

import jax
import jax.numpy as jnp
from jax import lax
from jax.experimental import pallas as pl
from jax.experimental.pallas import tpu as pltpu
from jax.sharding import PartitionSpec as P

MESH = pl.DeviceIdType.MESH
F32 = jnp.float32
BF16 = jnp.bfloat16
FIRST = 8
LAST = 15
PIECE = 48
CHUNKS = 12


def remote(src, dst, send_sem, recv_sem, device):
    return pltpu.make_async_remote_copy(
        src_ref=src,
        dst_ref=dst,
        send_sem=send_sem,
        recv_sem=recv_sem,
        device_id=device,
        device_id_type=MESH,
    )


def line_trees():
    paths = {
        0: [(0, 4, 9, 8), (9, 10), (0, 14, 15), (14, 13, 12, 11)],
        1: [(1, 8, 9, 10), (1, 14, 15), (14, 13, 12, 11)],
        2: [(2, 8, 9, 10), (2, 14, 15), (14, 13, 12, 11)],
        3: [(3, 9, 8), (9, 10, 11), (3, 14, 15), (14, 13, 12)],
        4: [(4, 9, 8), (9, 10, 11), (4, 14, 15), (14, 13, 12)],
        5: [(5, 9, 8), (9, 10, 11, 12), (5, 15, 14, 13)],
        6: [(6, 9, 8), (9, 10, 11, 12), (6, 15, 14, 13)],
        7: [(7, 9, 8), (9, 10, 11, 12), (7, 3, 14, 15), (14, 13)],
        8: [(8, 9, 10, 11, 12, 13), (8, 2, 15, 14)],
        9: [(9, 10, 11, 12, 13, 14), (9, 8, 2, 15)],
        10: [(10, 11, 12, 13, 14, 15), (10, 9, 8)],
        11: [(11, 12, 13, 14, 15), (11, 10, 9, 8)],
        12: [(12, 13, 14, 15), (12, 11, 10, 9, 8)],
        13: [(13, 14, 15), (13, 12, 11, 10, 9, 8)],
        14: [(14, 13, 12, 11, 10, 9), (14, 15, 5, 8)],
        15: [(15, 14, 13, 12, 11, 10), (15, 5, 8, 9)],
    }
    trees = []
    for s in range(16):
        parent = {}
        for path in paths[s]:
            for before, after in zip(path, path[1:]):
                assert after not in parent and after != s
                parent[after] = before
        trees.append(parent)
    return trees


def table_words(entries):
    return [
        sum(entries[s][4 * w + d] * 16**d for d in range(4)) for s in range(16) for w in range(4)
    ]


def tree_tables():
    none = [list(range(16)) for _ in range(16)]
    parents = [list(row) for row in none]
    firsts = [list(row) for row in none]
    seconds = [list(row) for row in none]
    for s, tree in enumerate(line_trees()):
        for plane, before in tree.items():
            parents[s][plane] = before
            if firsts[s][before] == before:
                firsts[s][before] = plane
            else:
                assert seconds[s][before] == before
                seconds[s][before] = plane
    return [table_words(entries) for entries in (parents, firsts, seconds)]


def look_up(words, s, z):
    index = s * 4 + z // 4
    word = words[0]
    for k, value in enumerate(words):
        if k:
            word = jnp.where(index == k, value, word)
    digit = z % 4
    scale = jnp.where(digit == 0, 1, jnp.where(digit == 1, 16, jnp.where(digit == 2, 256, 4096)))
    return (word // scale) % 16


def gather_kernel(ranks_ref, step_ref, left_ref, right_ref, panel_ref, sems):
    column = step_ref[0]
    slot = lax.rem(column, 3)

    @pl.when(lax.axis_index("col") == column // 3)
    def _():
        copies = [
            pltpu.make_async_copy(left_ref.at[:, slot], panel_ref.at[:, 0], sems.at[0]),
            pltpu.make_async_copy(right_ref.at[:, slot], panel_ref.at[:, 1], sems.at[1]),
        ]
        for copy in copies:
            copy.start()
        for copy in copies:
            copy.wait()
        level = lax.broadcasted_iota(jnp.int32, (96, 512), 0)
        for i in range(6):
            tile = panel_ref[i, 0]
            panel_ref[i, 0] = jnp.where(level < ranks_ref[slot, i], tile, jnp.zeros_like(tile))


def gather_panel(ranks, step, left, right):
    return pl.pallas_call(
        gather_kernel,
        out_shape=jax.ShapeDtypeStruct((6, 2, 96, 512), BF16),
        in_specs=[
            pl.BlockSpec(memory_space=pltpu.SMEM),
            pl.BlockSpec(memory_space=pltpu.SMEM),
            pl.BlockSpec(memory_space=pl.ANY),
            pl.BlockSpec(memory_space=pl.ANY),
        ],
        out_specs=pl.BlockSpec(memory_space=pltpu.VMEM),
        scratch_shapes=[pltpu.SemaphoreType.DMA((2,))],
        compiler_params=pltpu.CompilerParams(vmem_limit_bytes=62 * 2**20),
        name="gather_panel",
    )(ranks, step, left, right)


def panel_kernel(
    owner, panel_ref, out_ref, extra_ref, src_send, up_send, down_send, recv_sem,
    extra_up_send, extra_down_send, extra_recv, give_send, local_sem,
):
    z = lax.axis_index("row")
    c = lax.axis_index("col")
    s = c // 2
    kind = c % 2
    owner_line = owner // 2
    owner_core = owner % 2
    carrier = owner + 1 - 2 * owner_core
    home = z == s
    is_owner = c == owner
    is_carrier = c == carrier
    target = z >= FIRST
    parent, first, second = (look_up(words, s, z) for words in tree_tables())
    plain = jnp.logical_not(is_owner)
    up = plain & (first != z)
    down = plain & (second != z)
    from_owner = home & plain
    from_parent = plain & (parent != z)
    from_carrier = is_owner & target & (z != owner_line)
    receives = from_owner | from_parent | from_carrier
    sends_home = is_owner & (z != owner_line)
    holds_own = is_owner & (z == owner_line)
    extra_up = is_carrier & (first != z)
    extra_down = is_carrier & (second != z)
    extra_gives = is_carrier & target & (z != owner_line)
    extra_takes = is_carrier & (home | (parent != z))

    barrier = pltpu.get_barrier_semaphore()

    def greet(flag, device):
        @pl.when(flag)
        def _():
            pl.semaphore_signal(barrier, inc=1, device_id=device, device_id_type=MESH)

    greet(from_owner, (z, owner))
    greet(from_parent, (parent, c))
    greet(from_carrier, (z, carrier))

    def count(flag, amount=1):
        return jnp.where(flag, amount, 0)

    peers = (
        count(is_owner, jnp.where(z == owner_line, 1, 2))
        + count(up)
        + count(down)
        + count(extra_gives)
    )

    @pl.when(peers > 0)
    def _():
        pl.semaphore_wait(barrier, peers)

    def piece(q):
        return q // 4, (q // 2) % 2, pl.ds(pl.multiple_of((q % 2) * PIECE, PIECE), PIECE)

    def src_copy(core, q):
        t, side, rows = piece(q)
        return remote(
            panel_ref.at[3 * core + t, side, rows],
            out_ref.at[t, side, rows],
            src_send.at[core, q],
            recv_sem.at[q],
            (z, 2 * z + core),
        )

    def lend_copy(q):
        t, side, rows = piece(q)
        return remote(
            panel_ref.at[3 * owner_core + t, side, rows],
            extra_ref.at[t, side, rows],
            src_send.at[owner_core, q],
            extra_recv.at[q],
            (z, carrier),
        )

    def chain_copy(ref, send, recv, device, q):
        t, side, rows = piece(q)
        here = ref.at[t, side, rows]
        return remote(here, here, send.at[q], recv.at[q], device)

    def give_copy(q):
        t, side, rows = piece(q)
        return remote(
            extra_ref.at[t, side, rows], out_ref.at[t, side, rows], give_send.at[q], recv_sem.at[q], (z, owner)
        )

    def up_copy(q):
        return chain_copy(out_ref, up_send, recv_sem, (first, c), q)

    def down_copy(q):
        return chain_copy(out_ref, down_send, recv_sem, (second, c), q)

    def extra_up_copy(q):
        return chain_copy(extra_ref, extra_up_send, extra_recv, (first, c), q)

    def extra_down_copy(q):
        return chain_copy(extra_ref, extra_down_send, extra_recv, (second, c), q)

    def loop(flag, body):
        @pl.when(flag)
        def _():
            lax.fori_loop(0, CHUNKS, lambda q, _: (body(q), 0)[1], 0)

    loop(holds_own, lambda q: lend_copy(q).start())
    for core in range(2):
        flag = is_owner if core != owner_core else sends_home
        loop(flag, lambda q, core=core: src_copy(core, q).start())

    @pl.when(holds_own)
    def _():
        copy = pltpu.make_async_copy(panel_ref.at[pl.ds(3 * owner_core, 3)], out_ref, local_sem)
        copy.start()
        copy.wait()

    def relay(children, takes_extra=False, gives=False):
        def body(q):
            chain_copy(out_ref, up_send, recv_sem, (z, c + 1 - 2 * kind), q).wait_recv()
            if children > 0:
                up_copy(q).start()
            if children > 1:
                down_copy(q).start()
            if takes_extra:
                chain_copy(extra_ref, extra_up_send, extra_recv, (z, owner), q).wait_recv()
                if children > 0:
                    extra_up_copy(q).start()
                if children > 1:
                    extra_down_copy(q).start()
                if gives:
                    give_copy(q).start()

        return body

    roles = (jnp.logical_not(up), up & jnp.logical_not(down), down)
    common = receives & jnp.logical_not(extra_takes)
    for children, role in enumerate(roles):
        loop(common & role, relay(children))
        loop(extra_takes & extra_gives & role, relay(children, True, True))
        if children:
            loop(extra_takes & jnp.logical_not(extra_gives) & role, relay(children, True))

    loop(holds_own, lambda q: lend_copy(q).wait_send())
    for core in range(2):
        flag = is_owner if core != owner_core else sends_home
        loop(flag, lambda q, core=core: src_copy(core, q).wait_send())
    loop(up, lambda q: up_copy(q).wait_send())
    loop(down, lambda q: down_copy(q).wait_send())
    loop(extra_up, lambda q: extra_up_copy(q).wait_send())
    loop(extra_down, lambda q: extra_down_copy(q).wait_send())
    loop(extra_gives, lambda q: give_copy(q).wait_send())


def spread_panel(owner, panel):
    return pl.pallas_call(
        functools.partial(panel_kernel, owner),
        out_shape=jax.ShapeDtypeStruct((3, 2, 96, 512), BF16),
        in_specs=[pl.BlockSpec(memory_space=pltpu.VMEM)],
        out_specs=pl.BlockSpec(memory_space=pltpu.VMEM),
        scratch_shapes=[
            pltpu.VMEM((3, 2, 96, 512), BF16),
            pltpu.SemaphoreType.DMA((2, CHUNKS)),
            pltpu.SemaphoreType.DMA((CHUNKS,)),
            pltpu.SemaphoreType.DMA((CHUNKS,)),
            pltpu.SemaphoreType.DMA((CHUNKS,)),
            pltpu.SemaphoreType.DMA((CHUNKS,)),
            pltpu.SemaphoreType.DMA((CHUNKS,)),
            pltpu.SemaphoreType.DMA((CHUNKS,)),
            pltpu.SemaphoreType.DMA((CHUNKS,)),
            pltpu.SemaphoreType.DMA,
        ],
        compiler_params=pltpu.CompilerParams(
            collective_id=owner - 15, has_side_effects=True, vmem_limit_bytes=16 * 2**20
        ),
        name="spread_panel",
    )(panel)


def dot_nt(a, b):
    return lax.dot_general(a, b, (((1,), (1,)), ((), ())), preferred_element_type=F32)


def dot_nn(a, b):
    return jnp.dot(a, b, preferred_element_type=F32)


STARTS = (0, 3, 5)
SIZES = (3, 2, 1)
GROUPS = 3


def row_kernel(
    ranks_ref, step_ref, left_hbm, right_hbm, probe_hbm, upper_ref, sketch_ref, solve_ref, out_ref,
    left_ref, right_ref, probe_ref, reduced_ref,
    send_ref, got_ref, acc_ref, cur_ref, a_ref, b_ref,
    load_sem, send_sem, recv_sem, pair_send, pair_recv,
):
    z = lax.axis_index("row")
    c = lax.axis_index("col")
    x = c // 8
    y = (c // 2) % 4
    core = c % 2
    even = core == 0
    sibling = (z, c + 1 - 2 * core)
    u = jnp.where(even, x, y)
    v = jnp.where(even, y, x)

    def along_x(by):
        return ((x + by) % 4) * 8 + y * 2 + core

    def along_y(by):
        return x * 8 + ((y + by) % 4) * 2 + core

    firsts = [(z, jnp.where(even, along_x(by), along_y(by))) for by in (1, 2, 3)]
    seconds = [(z, jnp.where(even, along_y(by), along_x(by))) for by in (1, 2, 3)]

    def rows32(b):
        return pl.ds(pl.multiple_of(((b + 4) % 4) * 32, 32), 32)

    def members(g):
        return pl.ds(STARTS[g], SIZES[g])

    def copies(g, n, landing):
        made = []
        for k in range(3):
            by = k + 1
            if n == 0:
                src, dst = cur_ref.at[members(g), rows32(u + by)], a_ref.at[k, members(g)]
                if landing:
                    src = dst
            elif n == 1:
                src = dst = b_ref.at[(v - by + 4) % 4 if landing else v, members(g)]
            else:
                src = dst = out_ref.at[core, members(g), rows32(u - by if landing else u)]
            device = seconds[k] if n == 1 else firsts[k]
            made.append(remote(src, dst, send_sem.at[g, n, k], recv_sem.at[g, n, k], device))
        return made

    def start(g, n):
        for copy in copies(g, n, False):
            copy.start()

    def arrive(g, n):
        for copy in copies(g, n, True):
            copy.wait_recv()

    def pair_copy(g):
        rows = members(g)
        return remote(send_ref.at[rows], got_ref.at[rows], pair_send.at[0, g], pair_recv.at[0, g], sibling)

    def give_copy(g, which):
        here = out_ref.at[which, members(g)]
        return remote(here, here, pair_send.at[1, g], pair_recv.at[1, g], sibling)

    def loads(g):
        rows = members(g)
        return [
            pltpu.make_async_copy(left_hbm.at[rows], left_ref.at[rows], load_sem.at[0, g]),
            pltpu.make_async_copy(right_hbm.at[rows], right_ref.at[rows], load_sem.at[1, g]),
            pltpu.make_async_copy(probe_hbm.at[rows], probe_ref.at[rows], load_sem.at[2, g]),
        ]

    def compute(g):
        column = step_ref[0]
        for copy in loads(g):
            copy.wait()
        level = lax.broadcasted_iota(jnp.int32, (128, 96), 1)
        tiles = [c * 3 + j for j in range(3)]
        both = [
            dot_nt(right_ref[members(g), j].reshape(SIZES[g] * 96, 512), upper_ref[j, 0]) for j in range(3)
        ]
        for k in range(SIZES[g]):
            a = STARTS[g] + k
            part = slice(96 * k, 96 * (k + 1))
            live = z * 6 + a > column
            own_right = jnp.where(
                tiles[0] == column,
                right_ref[a, 0],
                jnp.where(tiles[1] == column, right_ref[a, 1], right_ref[a, 2]),
            )
            own_mixed = -dot_nn(own_right, sketch_ref[...]).T
            range_sum = jnp.zeros((128, 512), F32)
            co_sum = jnp.zeros((128, 512), F32)
            for j in range(3):
                own = tiles[j] == column
                depth = jnp.where(live & (tiles[j] <= column), ranks_ref[j, a], 0)
                keep = level < depth
                left = left_ref[a, j]
                coupled = both[j][part].astype(BF16)
                mixed = jnp.where(own, own_mixed, dot_nt(reduced_ref[j], coupled))
                mixed = jnp.where(keep, mixed, 0.0).astype(BF16)
                probed = dot_nt(probe_ref[a], left)
                probed = jnp.where(keep, probed, 0.0).astype(BF16)
                folded = dot_nn(probed, coupled).astype(BF16)
                folded = jnp.where(own, -probed, folded)
                closing = jnp.where(own, own_right, upper_ref[j, 1])
                range_sum += dot_nn(mixed, left)
                co_sum += dot_nn(folded, closing)
            acc_ref[a] = -jnp.where(even, range_sum, co_sum)
            send_ref[a] = -jnp.where(even, co_sum, range_sum).astype(BF16)
        pair_copy(g).start()

    def stage(n, g):
        rows = members(g)
        if n == 0:
            pair_copy(g).wait_recv()
            for by in range(4):
                block = rows32(u + by)
                total = acc_ref[rows, block] + got_ref[rows, block].astype(F32)
                if by:
                    cur_ref[rows, block] = total.astype(BF16)
                else:
                    acc_ref[rows, block] = total
            start(g, 0)
        elif n == 1:
            arrive(g, 0)
            total = acc_ref[rows, rows32(u)]
            for k in range(3):
                total += a_ref[k, rows].astype(F32)
            b_ref[v, rows] = total.astype(BF16)
            start(g, 1)
        elif n == 2:
            arrive(g, 1)
            total = b_ref[0, rows].astype(F32)
            for b in range(1, 4):
                total += b_ref[b, rows].astype(F32)
            block = total.astype(BF16)

            @pl.when(even)
            def _():
                out_ref[0, rows, rows32(u)] = block

            @pl.when(jnp.logical_not(even))
            def _():
                solved = dot_nn(block.reshape(SIZES[g] * 32, 512), solve_ref[...]).astype(BF16)
                out_ref[1, rows, rows32(u)] = solved.reshape(SIZES[g], 32, 512)

            start(g, 2)
        elif n == 3:
            arrive(g, 2)
            give_copy(g, core).start()
        else:
            give_copy(g, 1 - core).wait_recv()

    @pl.when(z < FIRST)
    def _():
        out_ref[...] = jnp.zeros_like(out_ref)

    @pl.when(z >= FIRST)
    def _():
        for g in range(GROUPS):
            for copy in loads(g):
                copy.start()
        barrier = pltpu.get_barrier_semaphore()
        for device in (sibling, *firsts, *seconds):
            pl.semaphore_signal(barrier, inc=1, device_id=device, device_id_type=MESH)
        for j in range(3):
            reduced = dot_nn(upper_ref[j, 1], sketch_ref[...]).astype(BF16).astype(F32)
            reduced_ref[j] = reduced.T.astype(BF16)
        pl.semaphore_wait(barrier, 7)

        for t in range(GROUPS + 5):
            if t < GROUPS:
                compute(t)
            for n in reversed(range(5)):
                if 0 <= t - 1 - n < GROUPS:
                    stage(n, t - 1 - n)
        for g in range(GROUPS):
            pair_copy(g).wait_send()
            give_copy(g, core).wait_send()
            for n in range(3):
                for copy in copies(g, n, False):
                    copy.wait_send()


def row_sums(ranks, step, left, right, probes, upper, sketch, solve):
    vmem = pl.BlockSpec(memory_space=pltpu.VMEM)
    smem = pl.BlockSpec(memory_space=pltpu.SMEM)
    hbm = pl.BlockSpec(memory_space=pl.ANY)
    return pl.pallas_call(
        row_kernel,
        out_shape=jax.ShapeDtypeStruct((2, 6, 128, 512), BF16),
        in_specs=[smem, smem, hbm, hbm, hbm, vmem, vmem, vmem],
        out_specs=vmem,
        scratch_shapes=[
            pltpu.VMEM((6, 3, 96, 512), BF16),
            pltpu.VMEM((6, 3, 96, 512), BF16),
            pltpu.VMEM((6, 128, 512), BF16),
            pltpu.VMEM((3, 128, 96), BF16),
            pltpu.VMEM((6, 128, 512), BF16),
            pltpu.VMEM((6, 128, 512), BF16),
            pltpu.VMEM((6, 128, 512), F32),
            pltpu.VMEM((6, 128, 512), BF16),
            pltpu.VMEM((3, 6, 32, 512), BF16),
            pltpu.VMEM((4, 6, 32, 512), BF16),
            pltpu.SemaphoreType.DMA((3, GROUPS)),
            pltpu.SemaphoreType.DMA((GROUPS, 3, 3)),
            pltpu.SemaphoreType.DMA((GROUPS, 3, 3)),
            pltpu.SemaphoreType.DMA((2, GROUPS)),
            pltpu.SemaphoreType.DMA((2, GROUPS)),
        ],
        compiler_params=pltpu.CompilerParams(
            collective_id=0, has_side_effects=True, vmem_limit_bytes=50 * 2**20
        ),
        name="row_sums",
    )(ranks, step, left, right, probes, upper, sketch, solve)


def body(left_factors, right_factors, ranks, sketch_left, sketch_right, upper_inverse, step):
    slots = ranks.T
    panel = gather_panel(slots, step, left_factors, right_factors)
    branches = [functools.partial(spread_panel, owner) for owner in range(16, 32)]
    upper = lax.switch(lax.div(step[0], 3) - 16, branches, panel)
    out = row_sums(
        slots, step, left_factors, right_factors, sketch_left, upper, sketch_right, upper_inverse
    )
    return (out[0], out[1])


def solution(mesh):
    return jax.shard_map(
        body,
        mesh=mesh,
        in_specs=(
            P("row", "col", None, None),
            P("row", "col", None, None),
            P("row", "col"),
            P("row", None, None),
            P(),
            P(),
            P(),
        ),
        out_specs=(P("row", None, None), P("row", None, None)),
        check_vma=False,
    )
```

```python
import functools

import jax
import jax.numpy as jnp
from jax import lax
from jax.experimental import pallas as pl
from jax.experimental.pallas import tpu as pltpu
from jax.sharding import PartitionSpec as P

MESH = pl.DeviceIdType.MESH
F32 = jnp.float32
BF16 = jnp.bfloat16
FIRST = 8
LAST = 15
PIECE = 48
CHUNKS = 12


def remote(src, dst, send_sem, recv_sem, device):
    return pltpu.make_async_remote_copy(
        src_ref=src,
        dst_ref=dst,
        send_sem=send_sem,
        recv_sem=recv_sem,
        device_id=device,
        device_id_type=MESH,
    )


def line_trees():
    paths = {
        0: [(0, 4, 9, 8), (9, 10), (0, 14, 15), (14, 13, 12, 11)],
        1: [(1, 8, 9, 10), (1, 14, 15), (14, 13, 12, 11)],
        2: [(2, 8, 9, 10), (2, 14, 15), (14, 13, 12, 11)],
        3: [(3, 9, 8), (9, 10, 11), (3, 14, 15), (14, 13, 12)],
        4: [(4, 9, 8), (9, 10, 11), (4, 14, 15), (14, 13, 12)],
        5: [(5, 9, 8), (9, 10, 11, 12), (5, 15, 14, 13)],
        6: [(6, 9, 8), (9, 10, 11, 12), (6, 15, 14, 13)],
        7: [(7, 9, 8), (9, 10, 11, 12), (7, 3, 14, 15), (14, 13)],
        8: [(8, 9, 10, 11, 12, 13), (8, 2, 15, 14)],
        9: [(9, 10, 11, 12, 13, 14), (9, 8, 2, 15)],
        10: [(10, 11, 12, 13, 14, 15), (10, 9, 8)],
        11: [(11, 12, 13, 14, 15), (11, 10, 9, 8)],
        12: [(12, 13, 14, 15), (12, 11, 10, 9, 8)],
        13: [(13, 14, 15), (13, 12, 11, 10, 9, 8)],
        14: [(14, 13, 12, 11, 10, 9), (14, 15, 5, 8)],
        15: [(15, 14, 13, 12, 11, 10), (15, 5, 8, 9)],
    }
    trees = []
    for s in range(16):
        parent = {}
        for path in paths[s]:
            for before, after in zip(path, path[1:]):
                assert after not in parent and after != s
                parent[after] = before
        trees.append(parent)
    return trees


def table_words(entries):
    return [
        sum(entries[s][4 * w + d] * 16**d for d in range(4)) for s in range(16) for w in range(4)
    ]


def tree_tables():
    none = [list(range(16)) for _ in range(16)]
    parents = [list(row) for row in none]
    firsts = [list(row) for row in none]
    seconds = [list(row) for row in none]
    for s, tree in enumerate(line_trees()):
        for plane, before in tree.items():
            parents[s][plane] = before
            if firsts[s][before] == before:
                firsts[s][before] = plane
            else:
                assert seconds[s][before] == before
                seconds[s][before] = plane
    return [table_words(entries) for entries in (parents, firsts, seconds)]


def look_up(words, s, z):
    index = s * 4 + z // 4
    word = words[0]
    for k, value in enumerate(words):
        if k:
            word = jnp.where(index == k, value, word)
    digit = z % 4
    scale = jnp.where(digit == 0, 1, jnp.where(digit == 1, 16, jnp.where(digit == 2, 256, 4096)))
    return (word // scale) % 16


def gather_kernel(ranks_ref, step_ref, left_ref, right_ref, panel_ref, sems):
    column = step_ref[0]
    slot = lax.rem(column, 3)

    @pl.when(lax.axis_index("col") == column // 3)
    def _():
        copies = [
            pltpu.make_async_copy(left_ref.at[:, slot], panel_ref.at[:, 0], sems.at[0]),
            pltpu.make_async_copy(right_ref.at[:, slot], panel_ref.at[:, 1], sems.at[1]),
        ]
        for copy in copies:
            copy.start()
        for copy in copies:
            copy.wait()
        level = lax.broadcasted_iota(jnp.int32, (96, 512), 0)
        for i in range(6):
            tile = panel_ref[i, 0]
            panel_ref[i, 0] = jnp.where(level < ranks_ref[slot, i], tile, jnp.zeros_like(tile))


def gather_panel(ranks, step, left, right):
    return pl.pallas_call(
        gather_kernel,
        out_shape=jax.ShapeDtypeStruct((6, 2, 96, 512), BF16),
        in_specs=[
            pl.BlockSpec(memory_space=pltpu.SMEM),
            pl.BlockSpec(memory_space=pltpu.SMEM),
            pl.BlockSpec(memory_space=pl.ANY),
            pl.BlockSpec(memory_space=pl.ANY),
        ],
        out_specs=pl.BlockSpec(memory_space=pltpu.VMEM),
        scratch_shapes=[pltpu.SemaphoreType.DMA((2,))],
        compiler_params=pltpu.CompilerParams(vmem_limit_bytes=62 * 2**20),
        name="gather_panel",
    )(ranks, step, left, right)


def panel_kernel(
    owner, panel_ref, out_ref, extra_ref, src_send, up_send, down_send, recv_sem,
    extra_up_send, extra_down_send, extra_recv, give_send, local_sem,
):
    z = lax.axis_index("row")
    c = lax.axis_index("col")
    s = c // 2
    kind = c % 2
    owner_line = owner // 2
    owner_core = owner % 2
    carrier = owner + 1 - 2 * owner_core
    home = z == s
    is_owner = c == owner
    is_carrier = c == carrier
    target = z >= FIRST
    parent, first, second = (look_up(words, s, z) for words in tree_tables())
    plain = jnp.logical_not(is_owner)
    up = plain & (first != z)
    down = plain & (second != z)
    from_owner = home & plain
    from_parent = plain & (parent != z)
    from_carrier = is_owner & target & (z != owner_line)
    receives = from_owner | from_parent | from_carrier
    sends_home = is_owner & (z != owner_line)
    holds_own = is_owner & (z == owner_line)
    extra_up = is_carrier & (first != z)
    extra_down = is_carrier & (second != z)
    extra_gives = is_carrier & target & (z != owner_line)
    extra_takes = is_carrier & (home | (parent != z))

    barrier = pltpu.get_barrier_semaphore()

    def greet(flag, device):
        @pl.when(flag)
        def _():
            pl.semaphore_signal(barrier, inc=1, device_id=device, device_id_type=MESH)

    greet(from_owner, (z, owner))
    greet(from_parent, (parent, c))
    greet(from_carrier, (z, carrier))

    def count(flag, amount=1):
        return jnp.where(flag, amount, 0)

    peers = (
        count(is_owner, jnp.where(z == owner_line, 1, 2))
        + count(up)
        + count(down)
        + count(extra_gives)
    )

    @pl.when(peers > 0)
    def _():
        pl.semaphore_wait(barrier, peers)

    def piece(q):
        return q // 4, (q // 2) % 2, pl.ds(pl.multiple_of((q % 2) * PIECE, PIECE), PIECE)

    def src_copy(core, q):
        t, side, rows = piece(q)
        return remote(
            panel_ref.at[3 * core + t, side, rows],
            out_ref.at[t, side, rows],
            src_send.at[core, q],
            recv_sem.at[q],
            (z, 2 * z + core),
        )

    def lend_copy(q):
        t, side, rows = piece(q)
        return remote(
            panel_ref.at[3 * owner_core + t, side, rows],
            extra_ref.at[t, side, rows],
            src_send.at[owner_core, q],
            extra_recv.at[q],
            (z, carrier),
        )

    def chain_copy(ref, send, recv, device, q):
        t, side, rows = piece(q)
        here = ref.at[t, side, rows]
        return remote(here, here, send.at[q], recv.at[q], device)

    def give_copy(q):
        t, side, rows = piece(q)
        return remote(
            extra_ref.at[t, side, rows], out_ref.at[t, side, rows], give_send.at[q], recv_sem.at[q], (z, owner)
        )

    def up_copy(q):
        return chain_copy(out_ref, up_send, recv_sem, (first, c), q)

    def down_copy(q):
        return chain_copy(out_ref, down_send, recv_sem, (second, c), q)

    def extra_up_copy(q):
        return chain_copy(extra_ref, extra_up_send, extra_recv, (first, c), q)

    def extra_down_copy(q):
        return chain_copy(extra_ref, extra_down_send, extra_recv, (second, c), q)

    def loop(flag, body):
        @pl.when(flag)
        def _():
            lax.fori_loop(0, CHUNKS, lambda q, _: (body(q), 0)[1], 0)

    loop(holds_own, lambda q: lend_copy(q).start())
    for core in range(2):
        flag = is_owner if core != owner_core else sends_home
        loop(flag, lambda q, core=core: src_copy(core, q).start())

    @pl.when(holds_own)
    def _():
        copy = pltpu.make_async_copy(panel_ref.at[pl.ds(3 * owner_core, 3)], out_ref, local_sem)
        copy.start()
        copy.wait()

    def relay(children, takes_extra=False, gives=False):
        def body(q):
            chain_copy(out_ref, up_send, recv_sem, (z, c + 1 - 2 * kind), q).wait_recv()
            if children > 0:
                up_copy(q).start()
            if children > 1:
                down_copy(q).start()
            if takes_extra:
                chain_copy(extra_ref, extra_up_send, extra_recv, (z, owner), q).wait_recv()
                if children > 0:
                    extra_up_copy(q).start()
                if children > 1:
                    extra_down_copy(q).start()
                if gives:
                    give_copy(q).start()

        return body

    roles = (jnp.logical_not(up), up & jnp.logical_not(down), down)
    common = receives & jnp.logical_not(extra_takes)
    for children, role in enumerate(roles):
        loop(common & role, relay(children))
        loop(extra_takes & extra_gives & role, relay(children, True, True))
        if children:
            loop(extra_takes & jnp.logical_not(extra_gives) & role, relay(children, True))

    loop(holds_own, lambda q: lend_copy(q).wait_send())
    for core in range(2):
        flag = is_owner if core != owner_core else sends_home
        loop(flag, lambda q, core=core: src_copy(core, q).wait_send())
    loop(up, lambda q: up_copy(q).wait_send())
    loop(down, lambda q: down_copy(q).wait_send())
    loop(extra_up, lambda q: extra_up_copy(q).wait_send())
    loop(extra_down, lambda q: extra_down_copy(q).wait_send())
    loop(extra_gives, lambda q: give_copy(q).wait_send())


def spread_panel(owner, panel):
    return pl.pallas_call(
        functools.partial(panel_kernel, owner),
        out_shape=jax.ShapeDtypeStruct((3, 2, 96, 512), BF16),
        in_specs=[pl.BlockSpec(memory_space=pltpu.VMEM)],
        out_specs=pl.BlockSpec(memory_space=pltpu.VMEM),
        scratch_shapes=[
            pltpu.VMEM((3, 2, 96, 512), BF16),
            pltpu.SemaphoreType.DMA((2, CHUNKS)),
            pltpu.SemaphoreType.DMA((CHUNKS,)),
            pltpu.SemaphoreType.DMA((CHUNKS,)),
            pltpu.SemaphoreType.DMA((CHUNKS,)),
            pltpu.SemaphoreType.DMA((CHUNKS,)),
            pltpu.SemaphoreType.DMA((CHUNKS,)),
            pltpu.SemaphoreType.DMA((CHUNKS,)),
            pltpu.SemaphoreType.DMA((CHUNKS,)),
            pltpu.SemaphoreType.DMA,
        ],
        compiler_params=pltpu.CompilerParams(
            collective_id=owner - 15, has_side_effects=True, vmem_limit_bytes=16 * 2**20
        ),
        name="spread_panel",
    )(panel)


def dot_nt(a, b):
    return lax.dot_general(a, b, (((1,), (1,)), ((), ())), preferred_element_type=F32)


def dot_nn(a, b):
    return jnp.dot(a, b, preferred_element_type=F32)


GROUP = 2
GROUPS = 6 // GROUP


def row_kernel(
    ranks_ref, step_ref, left_hbm, right_hbm, probe_hbm, upper_ref, sketch_ref, solve_ref, out_ref,
    left_ref, right_ref, probe_ref, reduced_ref,
    send_ref, got_ref, acc_ref, cur_ref, a_ref, b_ref,
    load_sem, send_sem, recv_sem, pair_send, pair_recv,
):
    z = lax.axis_index("row")
    c = lax.axis_index("col")
    x = c // 8
    y = (c // 2) % 4
    core = c % 2
    even = core == 0
    sibling = (z, c + 1 - 2 * core)
    u = jnp.where(even, x, y)
    v = jnp.where(even, y, x)

    def along_x(by):
        return ((x + by) % 4) * 8 + y * 2 + core

    def along_y(by):
        return x * 8 + ((y + by) % 4) * 2 + core

    firsts = [(z, jnp.where(even, along_x(by), along_y(by))) for by in (1, 2, 3)]
    seconds = [(z, jnp.where(even, along_y(by), along_x(by))) for by in (1, 2, 3)]

    def rows32(b):
        return pl.ds(pl.multiple_of(((b + 4) % 4) * 32, 32), 32)

    def members(g):
        return pl.ds(g * GROUP, GROUP)

    def copies(g, n, landing):
        made = []
        for k in range(3):
            by = k + 1
            if n == 0:
                src, dst = cur_ref.at[members(g), rows32(u + by)], a_ref.at[g, k]
                if landing:
                    src = dst
            elif n == 1:
                src = dst = b_ref.at[g, (v - by + 4) % 4 if landing else v]
            else:
                src = dst = out_ref.at[core, members(g), rows32(u - by if landing else u)]
            device = seconds[k] if n == 1 else firsts[k]
            made.append(remote(src, dst, send_sem.at[g, n, k], recv_sem.at[g, n, k], device))
        return made

    def start(g, n):
        for copy in copies(g, n, False):
            copy.start()

    def arrive(g, n):
        for copy in copies(g, n, True):
            copy.wait_recv()

    def pair_copy(g):
        rows = members(g)
        return remote(send_ref.at[rows], got_ref.at[rows], pair_send.at[0, g], pair_recv.at[0, g], sibling)

    def give_copy(g, which):
        here = out_ref.at[which, members(g)]
        return remote(here, here, pair_send.at[1, g], pair_recv.at[1, g], sibling)

    def loads(g):
        rows = members(g)
        return [
            pltpu.make_async_copy(left_hbm.at[rows], left_ref.at[rows], load_sem.at[0, g]),
            pltpu.make_async_copy(right_hbm.at[rows], right_ref.at[rows], load_sem.at[1, g]),
            pltpu.make_async_copy(probe_hbm.at[rows], probe_ref.at[rows], load_sem.at[2, g]),
        ]

    barrier = pltpu.get_barrier_semaphore()

    def compute(g):
        column = step_ref[0]
        for copy in loads(g):
            copy.wait()
        level = lax.broadcasted_iota(jnp.int32, (128, 96), 1)
        tiles = [c * 3 + j for j in range(3)]
        both = [
            dot_nt(right_ref[members(g), j].reshape(GROUP * 96, 512), upper_ref[j, 0]) for j in range(3)
        ]
        for k in range(GROUP):
            a = g * GROUP + k
            part = slice(96 * k, 96 * (k + 1))
            live = z * 6 + a > column
            own_right = jnp.where(
                tiles[0] == column,
                right_ref[a, 0],
                jnp.where(tiles[1] == column, right_ref[a, 1], right_ref[a, 2]),
            )
            own_mixed = -dot_nn(own_right, sketch_ref[...]).T
            range_sum = jnp.zeros((128, 512), F32)
            co_sum = jnp.zeros((128, 512), F32)
            for j in range(3):
                own = tiles[j] == column
                depth = jnp.where(live & (tiles[j] <= column), ranks_ref[j, a], 0)
                keep = level < depth
                left = left_ref[a, j]
                coupled = both[j][part].astype(BF16)
                mixed = jnp.where(own, own_mixed, dot_nt(reduced_ref[j], coupled))
                mixed = jnp.where(keep, mixed, 0.0).astype(BF16)
                probed = dot_nt(probe_ref[a], left)
                probed = jnp.where(keep, probed, 0.0).astype(BF16)
                folded = dot_nn(probed, coupled).astype(BF16)
                folded = jnp.where(own, -probed, folded)
                closing = jnp.where(own, own_right, upper_ref[j, 1])
                range_sum += dot_nn(mixed, left)
                co_sum += dot_nn(folded, closing)
            acc_ref[a] = -jnp.where(even, range_sum, co_sum)
            send_ref[a] = -jnp.where(even, co_sum, range_sum).astype(BF16)

        @pl.when(g == 0)
        def _():
            pl.semaphore_wait(barrier, 7)

        pair_copy(g).start()

    def stage(n, g):
        rows = members(g)
        if n == 0:
            pair_copy(g).wait_recv()
            for by in range(4):
                block = rows32(u + by)
                total = acc_ref[rows, block] + got_ref[rows, block].astype(F32)
                if by:
                    cur_ref[rows, block] = total.astype(BF16)
                else:
                    acc_ref[rows, block] = total
            start(g, 0)
        elif n == 1:
            arrive(g, 0)
            total = acc_ref[rows, rows32(u)]
            for k in range(3):
                total += a_ref[g, k].astype(F32)
            b_ref[g, v] = total.astype(BF16)
            start(g, 1)
        elif n == 2:
            arrive(g, 1)
            total = b_ref[g, 0].astype(F32)
            for b in range(1, 4):
                total += b_ref[g, b].astype(F32)
            block = total.astype(BF16)

            @pl.when(even)
            def _():
                out_ref[0, rows, rows32(u)] = block

            @pl.when(jnp.logical_not(even))
            def _():
                solved = dot_nn(block.reshape(GROUP * 32, 512), solve_ref[...]).astype(BF16)
                out_ref[1, rows, rows32(u)] = solved.reshape(GROUP, 32, 512)

            start(g, 2)
        elif n == 3:
            arrive(g, 2)
            give_copy(g, core).start()
        else:
            give_copy(g, 1 - core).wait_recv()

    @pl.when(z < FIRST)
    def _():
        out_ref[...] = jnp.zeros_like(out_ref)

    @pl.when(z >= FIRST)
    def _():
        for g in range(GROUPS):
            for copy in loads(g):
                copy.start()
        for device in (sibling, *firsts, *seconds):
            pl.semaphore_signal(barrier, inc=1, device_id=device, device_id_type=MESH)
        for j in range(3):
            reduced = dot_nn(upper_ref[j, 1], sketch_ref[...]).astype(BF16).astype(F32)
            reduced_ref[j] = reduced.T.astype(BF16)

        def slot(t, _):
            @pl.when(t < GROUPS)
            def _():
                compute(t)

            for n in reversed(range(5)):
                g = t - 1 - n

                @pl.when((g >= 0) & (g < GROUPS))
                def _(n=n, g=g):
                    stage(n, g)

            return 0

        lax.fori_loop(0, GROUPS + 5, slot, 0)

        def finish(g, _):
            pair_copy(g).wait_send()
            give_copy(g, core).wait_send()
            for n in range(3):
                for copy in copies(g, n, False):
                    copy.wait_send()
            return 0

        lax.fori_loop(0, GROUPS, finish, 0)


def row_sums(ranks, step, left, right, probes, upper, sketch, solve):
    vmem = pl.BlockSpec(memory_space=pltpu.VMEM)
    smem = pl.BlockSpec(memory_space=pltpu.SMEM)
    hbm = pl.BlockSpec(memory_space=pl.ANY)
    return pl.pallas_call(
        row_kernel,
        out_shape=jax.ShapeDtypeStruct((2, 6, 128, 512), BF16),
        in_specs=[smem, smem, hbm, hbm, hbm, vmem, vmem, vmem],
        out_specs=vmem,
        scratch_shapes=[
            pltpu.VMEM((6, 3, 96, 512), BF16),
            pltpu.VMEM((6, 3, 96, 512), BF16),
            pltpu.VMEM((6, 128, 512), BF16),
            pltpu.VMEM((3, 128, 96), BF16),
            pltpu.VMEM((6, 128, 512), BF16),
            pltpu.VMEM((6, 128, 512), BF16),
            pltpu.VMEM((6, 128, 512), F32),
            pltpu.VMEM((6, 128, 512), BF16),
            pltpu.VMEM((GROUPS, 3, GROUP, 32, 512), BF16),
            pltpu.VMEM((GROUPS, 4, GROUP, 32, 512), BF16),
            pltpu.SemaphoreType.DMA((3, GROUPS)),
            pltpu.SemaphoreType.DMA((GROUPS, 3, 3)),
            pltpu.SemaphoreType.DMA((GROUPS, 3, 3)),
            pltpu.SemaphoreType.DMA((2, GROUPS)),
            pltpu.SemaphoreType.DMA((2, GROUPS)),
        ],
        compiler_params=pltpu.CompilerParams(
            collective_id=0, has_side_effects=True, vmem_limit_bytes=50 * 2**20
        ),
        name="row_sums",
    )(ranks, step, left, right, probes, upper, sketch, solve)


def body(left_factors, right_factors, ranks, sketch_left, sketch_right, upper_inverse, step):
    slots = ranks.T
    panel = gather_panel(slots, step, left_factors, right_factors)
    branches = [functools.partial(spread_panel, owner) for owner in range(16, 32)]
    upper = lax.switch(lax.div(step[0], 3) - 16, branches, panel)
    out = row_sums(
        slots, step, left_factors, right_factors, sketch_left, upper, sketch_right, upper_inverse
    )
    return (out[0], out[1])


def solution(mesh):
    return jax.shard_map(
        body,
        mesh=mesh,
        in_specs=(
            P("row", "col", None, None),
            P("row", "col", None, None),
            P("row", "col"),
            P("row", None, None),
            P(),
            P(),
            P(),
        ),
        out_specs=(P("row", None, None), P("row", None, None)),
        check_vma=False,
    )
```

```python
import functools

import jax
import jax.numpy as jnp
from jax import lax
from jax.experimental import pallas as pl
from jax.experimental.pallas import tpu as pltpu
from jax.sharding import PartitionSpec as P

MESH = pl.DeviceIdType.MESH
F32 = jnp.float32
BF16 = jnp.bfloat16
FIRST = 8
LAST = 15
PIECE = 48
CHUNKS = 12


def remote(src, dst, send_sem, recv_sem, device):
    return pltpu.make_async_remote_copy(
        src_ref=src,
        dst_ref=dst,
        send_sem=send_sem,
        recv_sem=recv_sem,
        device_id=device,
        device_id_type=MESH,
    )


def line_trees():
    paths = {
        0: [(0, 4, 9, 8), (9, 10), (0, 14, 15), (14, 13, 12, 11)],
        1: [(1, 8, 9, 10), (1, 14, 15), (14, 13, 12, 11)],
        2: [(2, 8, 9, 10), (2, 14, 15), (14, 13, 12, 11)],
        3: [(3, 9, 8), (9, 10, 11), (3, 14, 15), (14, 13, 12)],
        4: [(4, 9, 8), (9, 10, 11), (4, 14, 15), (14, 13, 12)],
        5: [(5, 9, 8), (9, 10, 11, 12), (5, 15, 14, 13)],
        6: [(6, 9, 8), (9, 10, 11, 12), (6, 15, 14, 13)],
        7: [(7, 9, 8), (9, 10, 11, 12), (7, 3, 14, 15), (14, 13)],
        8: [(8, 9, 10, 11, 12, 13), (8, 2, 15, 14)],
        9: [(9, 10, 11, 12, 13, 14), (9, 8, 2, 15)],
        10: [(10, 11, 12, 13, 14, 15), (10, 9, 8)],
        11: [(11, 12, 13, 14, 15), (11, 10, 9, 8)],
        12: [(12, 13, 14, 15), (12, 11, 10, 9, 8)],
        13: [(13, 14, 15), (13, 12, 11, 10, 9, 8)],
        14: [(14, 13, 12, 11, 10, 9), (14, 15, 5, 8)],
        15: [(15, 14, 13, 12, 11, 10), (15, 5, 8, 9)],
    }
    trees = []
    for s in range(16):
        parent = {}
        for path in paths[s]:
            for before, after in zip(path, path[1:]):
                assert after not in parent and after != s
                parent[after] = before
        trees.append(parent)
    return trees


def table_words(entries):
    return [
        sum(entries[s][4 * w + d] * 16**d for d in range(4)) for s in range(16) for w in range(4)
    ]


def tree_tables():
    none = [list(range(16)) for _ in range(16)]
    parents = [list(row) for row in none]
    firsts = [list(row) for row in none]
    seconds = [list(row) for row in none]
    for s, tree in enumerate(line_trees()):
        for plane, before in tree.items():
            parents[s][plane] = before
            if firsts[s][before] == before:
                firsts[s][before] = plane
            else:
                assert seconds[s][before] == before
                seconds[s][before] = plane
    return [table_words(entries) for entries in (parents, firsts, seconds)]


def look_up(words, s, z):
    index = s * 4 + z // 4
    word = words[0]
    for k, value in enumerate(words):
        if k:
            word = jnp.where(index == k, value, word)
    digit = z % 4
    scale = jnp.where(digit == 0, 1, jnp.where(digit == 1, 16, jnp.where(digit == 2, 256, 4096)))
    return (word // scale) % 16


def gather_kernel(ranks_ref, step_ref, left_ref, right_ref, panel_ref, sems):
    column = step_ref[0]
    slot = lax.rem(column, 3)

    @pl.when(lax.axis_index("col") == column // 3)
    def _():
        copies = [
            pltpu.make_async_copy(left_ref.at[:, slot], panel_ref.at[:, 0], sems.at[0]),
            pltpu.make_async_copy(right_ref.at[:, slot], panel_ref.at[:, 1], sems.at[1]),
        ]
        for copy in copies:
            copy.start()
        for copy in copies:
            copy.wait()
        level = lax.broadcasted_iota(jnp.int32, (96, 512), 0)
        for i in range(6):
            tile = panel_ref[i, 0]
            panel_ref[i, 0] = jnp.where(level < ranks_ref[slot, i], tile, jnp.zeros_like(tile))


def gather_panel(ranks, step, left, right):
    return pl.pallas_call(
        gather_kernel,
        out_shape=jax.ShapeDtypeStruct((6, 2, 96, 512), BF16),
        in_specs=[
            pl.BlockSpec(memory_space=pltpu.SMEM),
            pl.BlockSpec(memory_space=pltpu.SMEM),
            pl.BlockSpec(memory_space=pl.ANY),
            pl.BlockSpec(memory_space=pl.ANY),
        ],
        out_specs=pl.BlockSpec(memory_space=pltpu.VMEM),
        scratch_shapes=[pltpu.SemaphoreType.DMA((2,))],
        compiler_params=pltpu.CompilerParams(vmem_limit_bytes=62 * 2**20),
        name="gather_panel",
    )(ranks, step, left, right)


def panel_kernel(
    owner, panel_ref, out_ref, extra_ref, src_send, up_send, down_send, recv_sem,
    extra_up_send, extra_down_send, extra_recv, give_send, local_sem,
):
    z = lax.axis_index("row")
    c = lax.axis_index("col")
    s = c // 2
    kind = c % 2
    owner_line = owner // 2
    owner_core = owner % 2
    carrier = owner + 1 - 2 * owner_core
    home = z == s
    is_owner = c == owner
    is_carrier = c == carrier
    target = z >= FIRST
    parent, first, second = (look_up(words, s, z) for words in tree_tables())
    plain = jnp.logical_not(is_owner)
    up = plain & (first != z)
    down = plain & (second != z)
    from_owner = home & plain
    from_parent = plain & (parent != z)
    from_carrier = is_owner & target & (z != owner_line)
    receives = from_owner | from_parent | from_carrier
    sends_home = is_owner & (z != owner_line)
    holds_own = is_owner & (z == owner_line)
    extra_up = is_carrier & (first != z)
    extra_down = is_carrier & (second != z)
    extra_gives = is_carrier & target & (z != owner_line)
    extra_takes = is_carrier & (home | (parent != z))

    barrier = pltpu.get_barrier_semaphore()

    def greet(flag, device):
        @pl.when(flag)
        def _():
            pl.semaphore_signal(barrier, inc=1, device_id=device, device_id_type=MESH)

    greet(from_owner, (z, owner))
    greet(from_parent, (parent, c))
    greet(from_carrier, (z, carrier))

    def count(flag, amount=1):
        return jnp.where(flag, amount, 0)

    peers = (
        count(is_owner, jnp.where(z == owner_line, 1, 2))
        + count(up)
        + count(down)
        + count(extra_gives)
    )

    @pl.when(peers > 0)
    def _():
        pl.semaphore_wait(barrier, peers)

    def piece(q):
        return q // 4, (q // 2) % 2, pl.ds(pl.multiple_of((q % 2) * PIECE, PIECE), PIECE)

    def src_copy(core, q):
        t, side, rows = piece(q)
        return remote(
            panel_ref.at[3 * core + t, side, rows],
            out_ref.at[t, side, rows],
            src_send.at[core, q],
            recv_sem.at[q],
            (z, 2 * z + core),
        )

    def lend_copy(q):
        t, side, rows = piece(q)
        return remote(
            panel_ref.at[3 * owner_core + t, side, rows],
            extra_ref.at[t, side, rows],
            src_send.at[owner_core, q],
            extra_recv.at[q],
            (z, carrier),
        )

    def chain_copy(ref, send, recv, device, q):
        t, side, rows = piece(q)
        here = ref.at[t, side, rows]
        return remote(here, here, send.at[q], recv.at[q], device)

    def give_copy(q):
        t, side, rows = piece(q)
        return remote(
            extra_ref.at[t, side, rows], out_ref.at[t, side, rows], give_send.at[q], recv_sem.at[q], (z, owner)
        )

    def up_copy(q):
        return chain_copy(out_ref, up_send, recv_sem, (first, c), q)

    def down_copy(q):
        return chain_copy(out_ref, down_send, recv_sem, (second, c), q)

    def extra_up_copy(q):
        return chain_copy(extra_ref, extra_up_send, extra_recv, (first, c), q)

    def extra_down_copy(q):
        return chain_copy(extra_ref, extra_down_send, extra_recv, (second, c), q)

    def loop(flag, body):
        @pl.when(flag)
        def _():
            lax.fori_loop(0, CHUNKS, lambda q, _: (body(q), 0)[1], 0)

    loop(holds_own, lambda q: lend_copy(q).start())
    for core in range(2):
        flag = is_owner if core != owner_core else sends_home
        loop(flag, lambda q, core=core: src_copy(core, q).start())

    @pl.when(holds_own)
    def _():
        copy = pltpu.make_async_copy(panel_ref.at[pl.ds(3 * owner_core, 3)], out_ref, local_sem)
        copy.start()
        copy.wait()

    def relay(children, takes_extra=False, gives=False):
        def body(q):
            chain_copy(out_ref, up_send, recv_sem, (z, c + 1 - 2 * kind), q).wait_recv()
            if children > 0:
                up_copy(q).start()
            if children > 1:
                down_copy(q).start()
            if takes_extra:
                chain_copy(extra_ref, extra_up_send, extra_recv, (z, owner), q).wait_recv()
                if children > 0:
                    extra_up_copy(q).start()
                if children > 1:
                    extra_down_copy(q).start()
                if gives:
                    give_copy(q).start()

        return body

    roles = (jnp.logical_not(up), up & jnp.logical_not(down), down)
    common = receives & jnp.logical_not(extra_takes)
    for children, role in enumerate(roles):
        loop(common & role, relay(children))
        loop(extra_takes & extra_gives & role, relay(children, True, True))
        if children:
            loop(extra_takes & jnp.logical_not(extra_gives) & role, relay(children, True))

    loop(holds_own, lambda q: lend_copy(q).wait_send())
    for core in range(2):
        flag = is_owner if core != owner_core else sends_home
        loop(flag, lambda q, core=core: src_copy(core, q).wait_send())
    loop(up, lambda q: up_copy(q).wait_send())
    loop(down, lambda q: down_copy(q).wait_send())
    loop(extra_up, lambda q: extra_up_copy(q).wait_send())
    loop(extra_down, lambda q: extra_down_copy(q).wait_send())
    loop(extra_gives, lambda q: give_copy(q).wait_send())


def spread_panel(owner, panel):
    return pl.pallas_call(
        functools.partial(panel_kernel, owner),
        out_shape=jax.ShapeDtypeStruct((3, 2, 96, 512), BF16),
        in_specs=[pl.BlockSpec(memory_space=pltpu.VMEM)],
        out_specs=pl.BlockSpec(memory_space=pltpu.VMEM),
        scratch_shapes=[
            pltpu.VMEM((3, 2, 96, 512), BF16),
            pltpu.SemaphoreType.DMA((2, CHUNKS)),
            pltpu.SemaphoreType.DMA((CHUNKS,)),
            pltpu.SemaphoreType.DMA((CHUNKS,)),
            pltpu.SemaphoreType.DMA((CHUNKS,)),
            pltpu.SemaphoreType.DMA((CHUNKS,)),
            pltpu.SemaphoreType.DMA((CHUNKS,)),
            pltpu.SemaphoreType.DMA((CHUNKS,)),
            pltpu.SemaphoreType.DMA((CHUNKS,)),
            pltpu.SemaphoreType.DMA,
        ],
        compiler_params=pltpu.CompilerParams(
            collective_id=owner - 15, has_side_effects=True, vmem_limit_bytes=16 * 2**20
        ),
        name="spread_panel",
    )(panel)


def dot_nt(a, b):
    return lax.dot_general(a, b, (((1,), (1,)), ((), ())), preferred_element_type=F32)


def dot_nn(a, b):
    return jnp.dot(a, b, preferred_element_type=F32)


GROUP = 2
GROUPS = 6 // GROUP


def row_kernel(
    ranks_ref, step_ref, left_hbm, right_hbm, probe_hbm, upper_ref, sketch_ref, solve_ref, out_ref,
    left_ref, right_ref, probe_ref, reduced_ref,
    send_ref, got_ref, acc_ref, cur_ref, a_ref, b_ref,
    load_sem, send_sem, recv_sem, pair_send, pair_recv,
):
    z = lax.axis_index("row")
    c = lax.axis_index("col")
    x = c // 8
    y = (c // 2) % 4
    core = c % 2
    even = core == 0
    sibling = (z, c + 1 - 2 * core)
    u = jnp.where(even, x, y)
    v = jnp.where(even, y, x)

    def along_x(by):
        return ((x + by) % 4) * 8 + y * 2 + core

    def along_y(by):
        return x * 8 + ((y + by) % 4) * 2 + core

    firsts = [(z, jnp.where(even, along_x(by), along_y(by))) for by in (1, 2, 3)]
    seconds = [(z, jnp.where(even, along_y(by), along_x(by))) for by in (1, 2, 3)]

    def rows32(b):
        return pl.ds(pl.multiple_of(((b + 4) % 4) * 32, 32), 32)

    def members(g):
        return pl.ds(g * GROUP, GROUP)

    def copies(g, n, landing):
        made = []
        for k in range(3):
            by = k + 1
            if n == 0:
                src, dst = cur_ref.at[members(g), rows32(u + by)], a_ref.at[g, k]
                if landing:
                    src = dst
            elif n == 1:
                src = dst = b_ref.at[g, (v - by + 4) % 4 if landing else v]
            else:
                src = dst = out_ref.at[core, members(g), rows32(u - by if landing else u)]
            device = seconds[k] if n == 1 else firsts[k]
            made.append(remote(src, dst, send_sem.at[g, n, k], recv_sem.at[g, n, k], device))
        return made

    def start(g, n):
        for copy in copies(g, n, False):
            copy.start()

    def arrive(g, n):
        for copy in copies(g, n, True):
            copy.wait_recv()

    def pair_copy(g):
        rows = members(g)
        return remote(send_ref.at[rows], got_ref.at[rows], pair_send.at[0, g], pair_recv.at[0, g], sibling)

    def give_copy(g, which):
        here = out_ref.at[which, members(g)]
        return remote(here, here, pair_send.at[1, g], pair_recv.at[1, g], sibling)

    def loads(g):
        rows = members(g)
        return [
            pltpu.make_async_copy(left_hbm.at[rows], left_ref.at[rows], load_sem.at[0, g]),
            pltpu.make_async_copy(right_hbm.at[rows], right_ref.at[rows], load_sem.at[1, g]),
            pltpu.make_async_copy(probe_hbm.at[rows], probe_ref.at[rows], load_sem.at[2, g]),
        ]

    barrier = pltpu.get_barrier_semaphore()

    def compute(g):
        column = step_ref[0]
        for copy in loads(g):
            copy.wait()
        level = lax.broadcasted_iota(jnp.int32, (128, 96), 1)
        tiles = [c * 3 + j for j in range(3)]

        def one_row(k, _):
            a = g * GROUP + k
            live = z * 6 + a > column
            own_right = jnp.where(
                tiles[0] == column,
                right_ref[a, 0],
                jnp.where(tiles[1] == column, right_ref[a, 1], right_ref[a, 2]),
            )
            own_mixed = -dot_nn(own_right, sketch_ref[...]).T
            range_sum = jnp.zeros((128, 512), F32)
            co_sum = jnp.zeros((128, 512), F32)
            for j in range(3):
                own = tiles[j] == column
                depth = jnp.where(live & (tiles[j] <= column), ranks_ref[j, a], 0)
                keep = level < depth
                left = left_ref[a, j]
                coupled = dot_nt(right_ref[a, j], upper_ref[j, 0]).astype(BF16)
                mixed = jnp.where(own, own_mixed, dot_nt(reduced_ref[j], coupled))
                mixed = jnp.where(keep, mixed, 0.0).astype(BF16)
                probed = dot_nt(probe_ref[a], left)
                probed = jnp.where(keep, probed, 0.0).astype(BF16)
                folded = dot_nn(probed, coupled).astype(BF16)
                folded = jnp.where(own, -probed, folded)
                closing = jnp.where(own, own_right, upper_ref[j, 1])
                range_sum += dot_nn(mixed, left)
                co_sum += dot_nn(folded, closing)
            acc_ref[a] = -jnp.where(even, range_sum, co_sum)
            send_ref[a] = -jnp.where(even, co_sum, range_sum).astype(BF16)
            return 0

        lax.fori_loop(0, GROUP, one_row, 0)

        @pl.when(g == 0)
        def _():
            pl.semaphore_wait(barrier, 7)

        pair_copy(g).start()

    def stage(n, g):
        rows = members(g)
        if n == 0:
            pair_copy(g).wait_recv()
            for by in range(4):
                block = rows32(u + by)
                total = acc_ref[rows, block] + got_ref[rows, block].astype(F32)
                if by:
                    cur_ref[rows, block] = total.astype(BF16)
                else:
                    acc_ref[rows, block] = total
            start(g, 0)
        elif n == 1:
            arrive(g, 0)
            total = acc_ref[rows, rows32(u)]
            for k in range(3):
                total += a_ref[g, k].astype(F32)
            b_ref[g, v] = total.astype(BF16)
            start(g, 1)
        elif n == 2:
            arrive(g, 1)
            total = b_ref[g, 0].astype(F32)
            for b in range(1, 4):
                total += b_ref[g, b].astype(F32)
            block = total.astype(BF16)

            @pl.when(even)
            def _():
                out_ref[0, rows, rows32(u)] = block

            @pl.when(jnp.logical_not(even))
            def _():
                solved = dot_nn(block.reshape(GROUP * 32, 512), solve_ref[...]).astype(BF16)
                out_ref[1, rows, rows32(u)] = solved.reshape(GROUP, 32, 512)

            start(g, 2)
        elif n == 3:
            arrive(g, 2)
            give_copy(g, core).start()
        else:
            give_copy(g, 1 - core).wait_recv()

    @pl.when(z < FIRST)
    def _():
        out_ref[...] = jnp.zeros_like(out_ref)

    @pl.when(z >= FIRST)
    def _():
        for g in range(GROUPS):
            for copy in loads(g):
                copy.start()
        for device in (sibling, *firsts, *seconds):
            pl.semaphore_signal(barrier, inc=1, device_id=device, device_id_type=MESH)
        for j in range(3):
            reduced = dot_nn(upper_ref[j, 1], sketch_ref[...]).astype(BF16).astype(F32)
            reduced_ref[j] = reduced.T.astype(BF16)

        def slot(t, _):
            @pl.when(t < GROUPS)
            def _():
                compute(t)

            for n in reversed(range(5)):
                g = t - 1 - n

                @pl.when((g >= 0) & (g < GROUPS))
                def _(n=n, g=g):
                    stage(n, g)

            return 0

        lax.fori_loop(0, GROUPS + 5, slot, 0)

        def finish(g, _):
            pair_copy(g).wait_send()
            give_copy(g, core).wait_send()
            for n in range(3):
                for copy in copies(g, n, False):
                    copy.wait_send()
            return 0

        lax.fori_loop(0, GROUPS, finish, 0)


def row_sums(ranks, step, left, right, probes, upper, sketch, solve):
    vmem = pl.BlockSpec(memory_space=pltpu.VMEM)
    smem = pl.BlockSpec(memory_space=pltpu.SMEM)
    hbm = pl.BlockSpec(memory_space=pl.ANY)
    return pl.pallas_call(
        row_kernel,
        out_shape=jax.ShapeDtypeStruct((2, 6, 128, 512), BF16),
        in_specs=[smem, smem, hbm, hbm, hbm, vmem, vmem, vmem],
        out_specs=vmem,
        scratch_shapes=[
            pltpu.VMEM((6, 3, 96, 512), BF16),
            pltpu.VMEM((6, 3, 96, 512), BF16),
            pltpu.VMEM((6, 128, 512), BF16),
            pltpu.VMEM((3, 128, 96), BF16),
            pltpu.VMEM((6, 128, 512), BF16),
            pltpu.VMEM((6, 128, 512), BF16),
            pltpu.VMEM((6, 128, 512), F32),
            pltpu.VMEM((6, 128, 512), BF16),
            pltpu.VMEM((GROUPS, 3, GROUP, 32, 512), BF16),
            pltpu.VMEM((GROUPS, 4, GROUP, 32, 512), BF16),
            pltpu.SemaphoreType.DMA((3, GROUPS)),
            pltpu.SemaphoreType.DMA((GROUPS, 3, 3)),
            pltpu.SemaphoreType.DMA((GROUPS, 3, 3)),
            pltpu.SemaphoreType.DMA((2, GROUPS)),
            pltpu.SemaphoreType.DMA((2, GROUPS)),
        ],
        compiler_params=pltpu.CompilerParams(
            collective_id=0, has_side_effects=True, vmem_limit_bytes=50 * 2**20
        ),
        name="row_sums",
    )(ranks, step, left, right, probes, upper, sketch, solve)


def body(left_factors, right_factors, ranks, sketch_left, sketch_right, upper_inverse, step):
    slots = ranks.T
    panel = gather_panel(slots, step, left_factors, right_factors)
    branches = [functools.partial(spread_panel, owner) for owner in range(16, 32)]
    upper = lax.switch(lax.div(step[0], 3) - 16, branches, panel)
    out = row_sums(
        slots, step, left_factors, right_factors, sketch_left, upper, sketch_right, upper_inverse
    )
    return (out[0], out[1])


def solution(mesh):
    return jax.shard_map(
        body,
        mesh=mesh,
        in_specs=(
            P("row", "col", None, None),
            P("row", "col", None, None),
            P("row", "col"),
            P("row", None, None),
            P(),
            P(),
            P(),
        ),
        out_specs=(P("row", None, None), P("row", None, None)),
        check_vma=False,
    )
```
